512 devices in a mesh: wave: 16 (over z), tile: 32 (over y, x, core).
Axes of the slice: x: 4, y: 4, z: 16, core: 2. Of those that a mesh axis runs over, the one named last changes fastest.
Arguments:
- warm_start: float32 [16, 2, 1024, 1024], P('wave', None, 'tile'), may hold values from -30 to 30
- class_map: int32 [1024, 1024], P('tile'), may hold values from 0 to 7
- conductivities: float32 [8], replicated, may hold values from 0.1 to 10
- wavenumbers: float32 [16], P('wave'), may hold values from 0.05 to 2
- weights: float32 [16], P('wave'), may hold values from 0.1 to 1
- source_row: int32 [2], replicated, may hold values from 0 to 1023
- source_col: int32 [2], replicated, may hold values from 0 to 1023
- electrode_row: int32 [64], replicated, may hold values from 0 to 1023
Outputs:
- potentials: float32 [2, 1024, 1024], P(None, 'tile', 'wave')
- readings: float32 [2, 64], replicated
The draws below stay inside these ranges and needn't reach their ends.
All inputs are finite; a program needn't handle non-finite values.
Results may differ from the reference program's by a relative error of at most 0.0003.
Values sent between devices are 32-bit elements; how exact they have to be, the bound alone decides.
A program may use at most 64 MiB of HBM per device.

```python
import math
import jax
import jax.numpy as jnp
from jax import lax

SRC = 2
NY = 1024
ITERS = 3
NCLASS = 8
NELEC = 64
NK = 16
NX = 1024


def draw_warm_start(key, part):
    first_key = jax.random.fold_in(key, 11)
    shape = (NK, SRC, NX, NY)
    row_frac = jnp.arange(NX, dtype=jnp.float32) / NX
    col_frac = jnp.arange(NY, dtype=jnp.float32) / NY
    values = jnp.clip(jax.random.normal(first_key, shape, jnp.float32), -5.0, 5.0)
    scale = jnp.power(10.0, row_frac - 0.5)[:, None] * jnp.power(10.0, 0.5 * col_frac - 0.25)[None, :]
    return values * scale[None, None]


def with_ends(drawn, rng, least, top_value):
    place = [jax.random.randint(jax.random.fold_in(rng, axis), (), 0, length) for axis, length in enumerate(drawn.shape)]
    widest = drawn.shape.index(max(drawn.shape))
    next_to = place[:widest] + [(place[widest] + 1) % drawn.shape[widest]] + place[widest + 1:]
    return drawn.at[tuple(place)].set(least).at[tuple(next_to)].set(top_value)


def level_of(own_key, extent, pieces, low, largest):
    def one(dim, shards_of):
        steps = jax.random.uniform(jax.random.fold_in(jax.random.fold_in(own_key, 6), dim), (shards_of,), jnp.float32, low / len(pieces), largest / len(pieces))
        return jnp.repeat(jnp.exp(steps), extent[dim] // shards_of).reshape((-1,) + (1,) * (len(extent) - dim - 1))

    level = one(*pieces[0])
    for cut in pieces[1:]:
        level = level * one(*cut)
    return level


def setup_inputs(seed: int = 0) -> dict:
    streams_of = jax.random.split(jax.random.key(seed), 9)
    warm_start = draw_warm_start(jax.random.fold_in(streams_of[8], 71), 0)
    class_map = with_ends(jax.random.randint(streams_of[1], (NX, NY), 0, NCLASS), jax.random.fold_in(streams_of[1], 1), 0, NCLASS - 1).astype(jnp.int32)
    conductivities = jnp.clip(jnp.exp(jax.random.uniform(streams_of[2], (NCLASS,), jnp.float32, math.log(0.1), math.log(10.0))), 0.1, 10.0)
    wavenumbers = jnp.clip(jnp.exp(math.log(2.0) - 3.6888794 * jax.random.uniform(streams_of[3], (NK,), jnp.float32) ** level_of(streams_of[3], (NK,), ((0, 16),), -0.2, 0.2)), 0.05, 2.0)
    weights = jnp.clip(jnp.exp(math.log(1.0) - 2.3025851 * jax.random.uniform(streams_of[4], (NK,), jnp.float32) ** level_of(streams_of[4], (NK,), ((0, 16),), -0.2, 0.2)), 0.1, 1.0)
    source_row = jax.random.randint(streams_of[5], (SRC,), 0, NX).astype(jnp.int32)
    source_col = jax.random.randint(streams_of[6], (SRC,), 0, NY).astype(jnp.int32)
    electrode_row = with_ends(jax.random.randint(streams_of[7], (NELEC,), 0, NX), jax.random.fold_in(streams_of[7], 1), 0, NX - 1).astype(jnp.int32)
    return {"warm_start": warm_start, "class_map": class_map, "conductivities": conductivities, "wavenumbers": wavenumbers, "weights": weights, "source_row": source_row, "source_col": source_col, "electrode_row": electrode_row}


source_strength = 50.0


def harmonic(left_val, right_val):
    return 2.0 * left_val * right_val / (left_val + right_val)


def reference(warm_start, class_map, conductivities, wavenumbers, weights, source_row, source_col, electrode_row):
    sigma = conductivities[class_map]
    sigma_pad = jnp.pad(sigma, ((1, 1), (0, 0)))
    face_row = harmonic(sigma_pad[:-1], sigma_pad[1:])
    face_up = face_row[:-1]
    face_down = face_row[1:]
    col_inner = harmonic(sigma[:, :-1], sigma[:, 1:])
    face_left = jnp.concatenate([jnp.zeros((NX, 1), jnp.float32), col_inner], axis=1)
    face_right = jnp.concatenate([col_inner, sigma[:, -1:]], axis=1)
    base = face_up + face_down + face_left + face_right
    row_ids = jnp.arange(NX, dtype=jnp.int32)
    col_ids = jnp.arange(NY, dtype=jnp.int32)
    hits = (row_ids[None, :, None] == source_row[:, None, None]) & (col_ids[None, None, :] == source_col[:, None, None])
    rhs = source_strength * hits.astype(jnp.float32)

    def one_wave(total, inputs):
        warm, wave_num, weight = inputs
        diag = base + (wave_num * wave_num) * sigma

        def operate(values):
            row_padded = jnp.pad(values, ((0, 0), (1, 1), (0, 0)))
            col_padded = jnp.pad(values, ((0, 0), (0, 0), (1, 1)))
            return (diag * values - face_up * row_padded[:, :-2] - face_down * row_padded[:, 2:]
                    - face_left * col_padded[:, :, :-2] - face_right * col_padded[:, :, 2:])

        def inner(first, second):
            return jnp.sum(first * second, axis=(1, 2))[:, None, None]

        field = warm
        residual = rhs - operate(field)
        scaled = residual / diag
        direction = scaled
        gamma_now = inner(residual, scaled)
        for iteration in range(ITERS):
            image = operate(direction)
            step_size = gamma_now / inner(direction, image)
            field = field + step_size * direction
            residual = residual - step_size * image
            scaled = residual / diag
            gamma_next = inner(residual, scaled)
            direction = scaled + (gamma_next / gamma_now) * direction
            gamma_now = gamma_next
        return total + weight * field, None

    potentials, _ = lax.scan(one_wave, jnp.zeros((SRC, NX, NY), jnp.float32), (warm_start, wavenumbers, weights))
    readings = potentials[:, electrode_row, 0]
    return potentials, readings
```

```python
import functools

import jax
import jax.numpy as jnp
from jax import lax
from jax.experimental import pallas as pl
from jax.experimental.pallas import tpu as pltpu
from jax.sharding import PartitionSpec as P

SOURCE_STRENGTH = 50.0
MESH = pl.DeviceIdType.MESH

WAVES = 16
TILES = 32
ROWS = 32
COLS = 1024
EXT = 40
LANES = 128

FIRST = {6: (5, 7, 8), -6: (-7, -5), 3: (2, 4), -3: (-4, -2), 0: (-1, 1)}
FIRST_LIST = [(c, o) for c, offsets in FIRST.items() for o in offsets]
SECOND_LIST = [c for c in FIRST if c != 0]


def harmonic(a, b):
    return 2.0 * a * b / (a + b)


def kernel(
    warm, cls, cond, wn, wt, srow, scol, erow,
    pot, read,
    xbuf, cbuf, ebuf, cond_s, wn_s, wt_s, srow_s, scol_s,
    halo_out, halo_in, pack_x, pack_y, slots_x, slots_y,
    chunks, got_first, sums, got_second, mine, slots_r,
    in_sem, halo_send, halo_recv, x_send, x_recv, y_send, y_recv,
    first_send, first_recv, second_send, second_recv, r_send, r_recv,
):
    w = lax.axis_index("wave")
    t = lax.axis_index("tile")

    loads = [
        pltpu.make_async_copy(cls, cbuf, in_sem.at[0]),
        pltpu.make_async_copy(cond, cond_s, in_sem.at[1]),
        pltpu.make_async_copy(warm.at[0], xbuf, in_sem.at[2]),
        pltpu.make_async_copy(wn, wn_s, in_sem.at[3]),
        pltpu.make_async_copy(wt, wt_s, in_sem.at[4]),
        pltpu.make_async_copy(srow, srow_s, in_sem.at[5]),
        pltpu.make_async_copy(scol, scol_s, in_sem.at[6]),
        pltpu.make_async_copy(erow, ebuf, in_sem.at[7]),
    ]
    for load in loads:
        load.start()

    below = lax.rem(t + 1, TILES)
    above = lax.rem(t + TILES - 1, TILES)
    group = t // 8
    place = lax.rem(t, 8)
    row_peers = [group * 8 + lax.rem(place + k, 8) for k in range(1, 8)]
    col_peers = [lax.rem(t + 8 * k, TILES) for k in range(1, 4)]
    wave_peers = [lax.rem(w + k, WAVES) for k in range(1, WAVES)]
    barrier = pltpu.get_barrier_semaphore()
    for peer in [below, above] + row_peers + col_peers:
        pl.semaphore_signal(barrier, inc=1, device_id=(w, peer), device_id_type=MESH)
    for peer in wave_peers:
        pl.semaphore_signal(barrier, inc=1, device_id=(peer, t), device_id_type=MESH)

    loads[0].wait()
    loads[1].wait()
    classes = cbuf[...]
    sigma = jnp.full((ROWS, COLS), cond_s[0], jnp.float32)
    for i in range(1, 8):
        sigma = jnp.where(classes == i, cond_s[i], sigma)
    for load in loads[2:]:
        load.wait()
    upper = lax.broadcasted_iota(jnp.int32, (8, COLS), 0) < 4
    upper_half = lax.broadcasted_iota(jnp.int32, (8, COLS // 2), 0) < 4
    half = COLS // 2
    halo_out[0, :, :COLS] = jnp.where(upper, xbuf[0, 0:8, :], pltpu.roll(xbuf[1, 0:8, :], 4, 0))
    halo_out[0, :, COLS:] = jnp.where(upper_half, sigma[0:8, :half], pltpu.roll(sigma[0:8, half:], 4, 0))
    halo_out[1, :, :COLS] = jnp.where(upper, pltpu.roll(xbuf[1, 24:32, :], 4, 0), xbuf[0, 24:32, :])
    halo_out[1, :, COLS:] = jnp.where(upper_half, pltpu.roll(sigma[24:32, half:], 4, 0), sigma[24:32, :half])

    pl.semaphore_wait(barrier, 2 + 7 + 3 + 15)

    def remote(src, dst, send, recv, device):
        return pltpu.make_async_remote_copy(
            src_ref=src, dst_ref=dst, send_sem=send, recv_sem=recv, device_id=device, device_id_type=MESH
        )

    halos = [
        remote(halo_out.at[0], halo_in.at[0], halo_send.at[0], halo_recv.at[0], (w, above)),
        remote(halo_out.at[1], halo_in.at[1], halo_send.at[1], halo_recv.at[1], (w, below)),
    ]
    for copy in halos:
        copy.start()
    for copy in halos:
        copy.wait_recv()

    from_below = halo_in[0]
    from_above = halo_in[1]
    sig_lo = jnp.where(upper_half, from_below[:, COLS:], from_above[:, COLS:])
    sig_hi = pltpu.roll(jnp.where(upper_half, from_above[:, COLS:], from_below[:, COLS:]), 4, 0)
    sig = jnp.concatenate([sigma, jnp.concatenate([sig_lo, sig_hi], axis=1)], axis=0)
    rim = (
        jnp.where(upper, from_below[:, :COLS], from_above[:, :COLS]),
        pltpu.roll(jnp.where(upper, from_above[:, :COLS], from_below[:, :COLS]), 4, 0),
    )

    ext_row = lax.broadcasted_iota(jnp.int32, (EXT, COLS), 0)
    col = lax.broadcasted_iota(jnp.int32, (EXT, COLS), 1)
    closed = jnp.where(t == TILES - 1, ROWS - 1, -1)
    closed_top = jnp.where(t == 0, EXT - 1, -1)

    def down(v):
        return pltpu.roll(v, EXT - 1, 0)

    def up(v):
        return pltpu.roll(v, 1, 0)

    def right(v):
        return pltpu.roll(v, COLS - 1, 1)

    def left(v):
        return pltpu.roll(v, 1, 1)

    face_down = harmonic(sig, down(sig))
    face_down = jnp.where((ext_row == closed) | (ext_row == closed_top), 0.0, face_down)
    face_up = up(face_down)
    last = col == COLS - 1
    face_right = jnp.where(last, 0.0, harmonic(sig, right(sig)))
    face_left = left(face_right)
    k = wn_s[0]
    diag = face_up + face_down + face_left + face_right + jnp.where(last, sig, 0.0) + (k * k) * sig
    inv = 1.0 / diag
    a_up = face_up * inv
    a_down = face_down * inv
    a_left = face_left * inv
    a_right = face_right * inv

    def apply(v):
        return a_up * up(v) + a_down * down(v) + a_left * left(v) + a_right * right(v)

    global_row = jnp.where(ext_row < ROWS + 4, ext_row, ext_row - EXT) + t * ROWS
    d_own = diag[:ROWS]

    def fold(product):
        total = product[:, :LANES]
        for j in range(1, COLS // LANES):
            total = total + product[:, j * LANES:(j + 1) * LANES]
        return jnp.sum(total, axis=0, keepdims=True)

    lane = lax.broadcasted_iota(jnp.int32, (1, LANES), 1)
    vectors = []
    moments = []
    for s in range(2):
        x = jnp.concatenate([xbuf[s], rim[s]], axis=0)
        q = jnp.where((global_row == srow_s[s]) & (col == scol_s[s]), SOURCE_STRENGTH, 0.0)
        v0 = q * inv - x + apply(x)
        v1 = apply(v0)
        v2 = apply(v1)
        v3 = apply(v2)[:ROWS]
        v0, v1, v2 = v0[:ROWS], v1[:ROWS], v2[:ROWS]
        d0, d1, d2 = d_own * v0, d_own * v1, d_own * v2
        moments += [fold(d0 * v0), fold(d0 * v1), fold(d1 * v1), fold(d1 * v2), fold(d2 * v2), fold(d2 * v3)]
        vectors.append((xbuf[s], v0, v1, v2))

    electrode = ebuf[...].reshape(1, 64)
    electrode = jnp.concatenate([electrode, electrode], axis=1)
    here = lax.broadcasted_iota(jnp.int32, (ROWS, LANES), 0) + t * ROWS == electrode
    low = lane < 64
    surface = []
    for i in range(4):
        both = jnp.where(low, vectors[0][i][:, 0:1], vectors[1][i][:, 0:1])
        surface.append(jnp.sum(jnp.where(here, both, 0.0), axis=0, keepdims=True))

    pack_x[...] = jnp.concatenate(moments + surface, axis=0)
    copies_x = [
        remote(pack_x, slots_x.at[i], x_send.at[i], x_recv.at[i], (w, peer)) for i, peer in enumerate(row_peers)
    ]
    for copy in copies_x:
        copy.start()
    total = pack_x[...]
    for i, copy in enumerate(copies_x):
        copy.wait_recv()
        total = total + slots_x[i]
    pack_y[...] = total
    copies_y = [
        remote(pack_y, slots_y.at[i], y_send.at[i], y_recv.at[i], (w, peer)) for i, peer in enumerate(col_peers)
    ]
    for copy in copies_y:
        copy.start()
    for i, copy in enumerate(copies_y):
        copy.wait_recv()
        total = total + slots_y[i]
    dots = jnp.sum(total, axis=1, keepdims=True)

    weight = wt_s[0]
    coefs = []
    for s in range(2):
        nu = [jnp.broadcast_to(dots[6 * s + m:6 * s + m + 1], (1, LANES)) for m in range(6)]
        mu = [nu[m] - nu[m + 1] for m in range(5)]
        gamma0 = nu[0]
        alpha0 = gamma0 / mu[0]
        za, zb = 1.0 - alpha0, alpha0
        gamma1 = za * za * nu[0] + 2.0 * za * zb * nu[1] + zb * zb * nu[2]
        beta0 = gamma1 / gamma0
        pa, pb = za + beta0, zb
        curve1 = pa * pa * mu[0] + 2.0 * pa * pb * mu[1] + pb * pb * mu[2]
        alpha1 = gamma1 / curve1
        ya, yb, yc = za - alpha1 * pa, zb - alpha1 * (pb - pa), alpha1 * pb
        gamma2 = (
            ya * ya * nu[0] + yb * yb * nu[2] + yc * yc * nu[4]
            + 2.0 * (ya * yb * nu[1] + ya * yc * nu[2] + yb * yc * nu[3])
        )
        beta1 = gamma2 / gamma1
        ra, rb, rc = ya + beta1 * pa, yb + beta1 * pb, yc
        curve2 = (
            ra * ra * mu[0] + rb * rb * mu[2] + rc * rc * mu[4]
            + 2.0 * (ra * rb * mu[1] + ra * rc * mu[2] + rb * rc * mu[3])
        )
        alpha2 = gamma2 / curve2
        coefs.append((
            jnp.full((1, LANES), weight, jnp.float32),
            weight * (alpha0 + alpha1 * pa + alpha2 * ra),
            weight * (alpha1 * pb + alpha2 * rb),
            weight * (alpha2 * rc),
        ))

    low_rows = lax.broadcasted_iota(jnp.int32, (ROWS, LANES), 1) < 64
    for j in range(COLS // LANES):
        part = []
        for s in range(2):
            acc = vectors[s][0][:, j * LANES:(j + 1) * LANES] * coefs[s][0]
            for i in range(1, 4):
                acc = acc + vectors[s][i][:, j * LANES:(j + 1) * LANES] * coefs[s][i]
            part.append(acc)
        chunks[2 * j] = jnp.where(low_rows, part[0], pltpu.roll(part[1], 64, 1))
        chunks[2 * j + 1] = jnp.where(low_rows, pltpu.roll(part[0], 64, 1), part[1])

    def owner(offset):
        return lax.rem(w + 2 * WAVES - offset, WAVES)

    copies_first = [
        remote(
            chunks.at[owner(o)], got_first.at[i], first_send.at[i], first_recv.at[i],
            (lax.rem(w + 2 * WAVES + c - o, WAVES), t),
        )
        for i, (c, o) in enumerate(FIRST_LIST)
    ]
    for copy in copies_first:
        copy.start()

    mine[...] = sum(
        surface_total * jnp.where(low, coefs[0][i], coefs[1][i])
        for i, surface_total in enumerate([total[12 + i:13 + i] for i in range(4)])
    )
    copies_r = [
        remote(mine, slots_r.at[i], r_send.at[i], r_recv.at[i], (peer, t)) for i, peer in enumerate(wave_peers)
    ]
    for copy in copies_r:
        copy.start()

    copies_second = []
    for j, c in enumerate(SECOND_LIST):
        acc = chunks[owner(c)]
        for i, (cc, o) in enumerate(FIRST_LIST):
            if cc == c:
                copies_first[i].wait_recv()
                acc = acc + got_first[i]
        sums[j] = acc
        copy = remote(
            sums.at[j], got_second.at[j], second_send.at[j], second_recv.at[j], (owner(c), t)
        )
        copy.start()
        copies_second.append(copy)

    out_r = mine[...]
    for i, copy in enumerate(copies_r):
        copy.wait_recv()
        out_r = out_r + slots_r[i]
    read[0:1, :] = out_r[:, :64]
    read[1:2, :] = out_r[:, 64:]

    acc = chunks[w]
    for i, (c, o) in enumerate(FIRST_LIST):
        if c == 0:
            copies_first[i].wait_recv()
            acc = acc + got_first[i]
    for j, copy in enumerate(copies_second):
        copy.wait_recv()
        acc = acc + got_second[j]
    pot[0] = acc[:, :64]
    pot[1] = acc[:, 64:]

    for copy in halos + copies_x + copies_y + copies_first + copies_r + copies_second:
        copy.wait_send()


def shards(warm, cls, cond, wn, wt, srow, scol, erow):
    f32 = jnp.float32
    dma = pltpu.SemaphoreType.DMA
    n_first, n_second = len(FIRST_LIST), len(SECOND_LIST)
    return pl.pallas_call(
        kernel,
        out_shape=(
            jax.ShapeDtypeStruct((2, ROWS, COLS // WAVES), f32),
            jax.ShapeDtypeStruct((2, 64), f32),
        ),
        in_specs=[pl.BlockSpec(memory_space=pl.ANY)] * 8,
        out_specs=[pl.BlockSpec(memory_space=pltpu.VMEM)] * 2,
        scratch_shapes=[
            pltpu.VMEM((2, ROWS, COLS), f32),
            pltpu.VMEM((ROWS, COLS), jnp.int32),
            pltpu.VMEM((64,), jnp.int32),
            pltpu.SMEM((8,), f32),
            pltpu.SMEM((1,), f32),
            pltpu.SMEM((1,), f32),
            pltpu.SMEM((2,), jnp.int32),
            pltpu.SMEM((2,), jnp.int32),
            pltpu.VMEM((2, 8, COLS + COLS // 2), f32),
            pltpu.VMEM((2, 8, COLS + COLS // 2), f32),
            pltpu.VMEM((16, LANES), f32),
            pltpu.VMEM((16, LANES), f32),
            pltpu.VMEM((7, 16, LANES), f32),
            pltpu.VMEM((3, 16, LANES), f32),
            pltpu.VMEM((WAVES, ROWS, LANES), f32),
            pltpu.VMEM((n_first, ROWS, LANES), f32),
            pltpu.VMEM((n_second, ROWS, LANES), f32),
            pltpu.VMEM((n_second, ROWS, LANES), f32),
            pltpu.VMEM((1, LANES), f32),
            pltpu.VMEM((WAVES - 1, 1, LANES), f32),
            dma((8,)),
            dma((2,)), dma((2,)),
            dma((7,)), dma((7,)),
            dma((3,)), dma((3,)),
            dma((n_first,)), dma((n_first,)),
            dma((n_second,)), dma((n_second,)),
            dma((WAVES - 1,)), dma((WAVES - 1,)),
        ],
        compiler_params=pltpu.CompilerParams(
            collective_id=0, has_side_effects=True, vmem_limit_bytes=40 * 1024 * 1024
        ),
    )(warm, cls, cond, wn, wt, srow, scol, erow)


def solution(mesh):
    return jax.shard_map(
        shards,
        mesh=mesh,
        in_specs=(
            P("wave", None, "tile", None), P("tile", None), P(), P("wave"), P("wave"), P(), P(), P(),
        ),
        out_specs=(P(None, "tile", "wave"), P()),
        check_vma=False,
    )
```

```python
import jax
import jax.numpy as jnp
from jax import lax
from jax.experimental import pallas as pl
from jax.experimental.pallas import tpu as pltpu
from jax.sharding import PartitionSpec as P

SOURCE_STRENGTH = 50.0
MESH = pl.DeviceIdType.MESH

WAVES = 16
TILES = 32
ROWS = 32
COLS = 1024
LANES = 128
HALF = COLS // 2

FIRST = {7: (6, 8), -7: (-6,), 4: (3, 5), -4: (-3, -5), 2: (1,), -2: (-1,)}
FIRST_LIST = [(c, o) for c, offsets in FIRST.items() for o in offsets]
SECOND_LIST = list(FIRST)

STEPS = sorted(
    [(a, b, c) for a in range(4) for b in range(4) for c in range(2) if (a, b, c) != (0, 0, 0)],
    key=lambda s: -(min(s[0], 4 - s[0]) + min(s[1], 4 - s[1])),
)
NEAR = [s for s in STEPS if min(s[0], 4 - s[0]) + min(s[1], 4 - s[1]) <= 1]
FAR = [s for s in STEPS if min(s[0], 4 - s[0]) + min(s[1], 4 - s[1]) == 2 and s[2] == 0]


def harmonic(a, b):
    return 2.0 * a * b / (a + b)


def right(v):
    return pltpu.roll(v, COLS - 1, 1)


def left(v):
    return pltpu.roll(v, 1, 1)


def kernel(
    warm, cls, cond, wn, wt, srow, scol, erow,
    pot, read,
    xbuf, cbuf, ebuf, cond_s, wn_s, wt_s, srow_s, scol_s,
    halo_out, halo_in, packet, slots,
    chunks, got_first, sums, got_second, mine, slots_r,
    in_sem, halo_send, halo_recv, tile_send, tile_recv,
    first_send, first_recv, second_send, second_recv, r_send, r_recv,
    known,
):
    w = lax.axis_index("wave")
    t = lax.axis_index("tile")

    loads = [
        pltpu.make_async_copy(cls, cbuf, in_sem.at[0]),
        pltpu.make_async_copy(cond, cond_s, in_sem.at[1]),
        pltpu.make_async_copy(warm.at[0], xbuf, in_sem.at[2]),
        pltpu.make_async_copy(wn, wn_s, in_sem.at[3]),
        pltpu.make_async_copy(wt, wt_s, in_sem.at[4]),
        pltpu.make_async_copy(srow, srow_s, in_sem.at[5]),
        pltpu.make_async_copy(scol, scol_s, in_sem.at[6]),
        pltpu.make_async_copy(erow, ebuf, in_sem.at[7]),
    ]
    for load in loads:
        load.start()

    below = lax.rem(t + 1, TILES)
    above = lax.rem(t + TILES - 1, TILES)
    t_y, t_x, t_core = t // 8, lax.rem(t // 2, 4), lax.rem(t, 2)

    def tile_peer(step):
        dy, dx, dc = step
        return (w, lax.rem(t_y + dy, 4) * 8 + lax.rem(t_x + dx, 4) * 2 + lax.rem(t_core + dc, 2))

    def wave_peer(k):
        return (lax.rem(w + 2 * WAVES + k, WAVES), t)

    def tell(semaphore, peers):
        for peer in peers:
            pl.semaphore_signal(semaphore, inc=1, device_id=peer, device_id_type=MESH)

    near = [(w, below), (w, above)] + [tile_peer(s) for s in NEAR] + [wave_peer(1), wave_peer(-1)]
    middle = [tile_peer(s) for s in FAR] + [wave_peer(2), wave_peer(-2)]
    far = [wave_peer(4), wave_peer(-4)]
    barrier = pltpu.get_barrier_semaphore()
    tell(barrier, near)

    loads[0].wait()
    loads[1].wait()
    classes = cbuf[...]
    sigma = jnp.full((ROWS, COLS), cond_s[0], jnp.float32)
    for i in range(1, 8):
        sigma = jnp.where(classes == i, cond_s[i], sigma)
    for load in loads[2:]:
        load.wait()
    upper = lax.broadcasted_iota(jnp.int32, (8, COLS), 0) < 4
    upper_half = lax.broadcasted_iota(jnp.int32, (8, HALF), 0) < 4
    halo_out[0, :, :COLS] = jnp.where(upper, xbuf[0, 0:8, :], pltpu.roll(xbuf[1, 0:8, :], 4, 0))
    halo_out[0, :, COLS:] = jnp.where(upper_half, sigma[0:8, :HALF], pltpu.roll(sigma[0:8, HALF:], 4, 0))
    halo_out[1, :, :COLS] = jnp.where(upper, pltpu.roll(xbuf[1, 24:32, :], 4, 0), xbuf[0, 24:32, :])
    halo_out[1, :, COLS:] = jnp.where(upper_half, pltpu.roll(sigma[24:32, HALF:], 4, 0), sigma[24:32, :HALF])

    pl.semaphore_wait(barrier, len(near))

    def remote(src, dst, send, recv, device):
        return pltpu.make_async_remote_copy(
            src_ref=src, dst_ref=dst, send_sem=send, recv_sem=recv, device_id=device, device_id_type=MESH
        )

    halos = [
        remote(halo_out.at[0], halo_in.at[0], halo_send.at[0], halo_recv.at[0], (w, above)),
        remote(halo_out.at[1], halo_in.at[1], halo_send.at[1], halo_recv.at[1], (w, below)),
    ]
    for copy in halos:
        copy.start()
    tell(known.at[0], near)

    k = wn_s[0]

    def stencil(sig, cell_row, up, down, closed):
        shape = sig.shape
        row = lax.broadcasted_iota(jnp.int32, shape, 0)
        col = lax.broadcasted_iota(jnp.int32, shape, 1)
        last = col == COLS - 1
        face_down = harmonic(sig, down(sig, 0))
        face_up = harmonic(sig, up(sig, 0))
        if closed is not None:
            face_down = jnp.where(closed[1](row), 0.0, face_down)
            face_up = jnp.where(closed[0](row), 0.0, face_up)
        face_right = jnp.where(last, 0.0, harmonic(sig, right(sig)))
        face_left = left(face_right)
        diag = face_up + face_down + face_left + face_right + jnp.where(last, sig, 0.0) + (k * k) * sig
        inv = 1.0 / diag
        a_up, a_down, a_left, a_right = face_up * inv, face_down * inv, face_left * inv, face_right * inv

        def apply(v, tag):
            return a_up * up(v, tag) + a_down * down(v, tag) + a_left * left(v) + a_right * right(v)

        def chain(x, s):
            q = jnp.where((cell_row(row) + t * ROWS == srow_s[s]) & (col == scol_s[s]), SOURCE_STRENGTH, 0.0)
            v0 = q * inv - x + apply(x, (s, 0))
            v1 = apply(v0, (s, 1))
            v2 = apply(v1, (s, 2))
            return v0, v1, v2, apply(v2, (s, 3))

        return diag, chain

    def fold(product):
        total = product[:, :LANES]
        for j in range(1, COLS // LANES):
            total = total + product[:, j * LANES:(j + 1) * LANES]
        return jnp.sum(total, axis=0, keepdims=True)

    def moments(d, v0, v1, v2, v3):
        d0, d1, d2 = d * v0, d * v1, d * v2
        return [fold(a * b) for a, b in ((d0, v0), (d0, v1), (d1, v1), (d1, v2), (d2, v2), (d2, v3))]

    diag, chain = stencil(
        sigma,
        lambda row: row,
        lambda v, tag: pltpu.roll(v, 1, 0),
        lambda v, tag: pltpu.roll(v, ROWS - 1, 0),
        None,
    )
    inner = [chain(xbuf[s], s) for s in range(2)]
    inner_moments = [moments(diag[8:24], *[v[8:24] for v in inner[s]]) for s in range(2)]

    electrode = ebuf[...].reshape(1, 64)
    electrode = jnp.concatenate([electrode, electrode], axis=1)
    here = lax.broadcasted_iota(jnp.int32, (ROWS, LANES), 0) + t * ROWS == electrode

    for copy in halos:
        copy.wait_recv()
    pl.semaphore_wait(known.at[0], len(near))
    tell(known.at[1], middle)

    from_below = halo_in[0]
    from_above = halo_in[1]
    sig_lo = jnp.where(upper_half, from_below[:, COLS:], from_above[:, COLS:])
    sig_hi = pltpu.roll(jnp.where(upper_half, from_above[:, COLS:], from_below[:, COLS:]), 4, 0)
    rim_sigma = jnp.concatenate([sig_lo, sig_hi], axis=1)
    rim = (
        jnp.where(upper, from_below[:, :COLS], from_above[:, :COLS]),
        pltpu.roll(jnp.where(upper, from_above[:, :COLS], from_below[:, :COLS]), 4, 0),
    )
    own = {0: sigma}
    for s in range(2):
        own[(s, 0)] = xbuf[s]
        for i in range(3):
            own[(s, i + 1)] = inner[s][i]

    def strip(v, middle_rows):
        return jnp.concatenate([v[24:32], middle_rows, v[0:8]], axis=0)

    def strip_up(v, tag):
        return pltpu.roll(jnp.concatenate([own[tag][16:24], v], axis=0), 1, 0)[8:]

    def strip_down(v, tag):
        return pltpu.roll(jnp.concatenate([v, own[tag][8:16]], axis=0), 31, 0)[:24]

    bottom = jnp.where(t == TILES - 1, 0, 100)
    top = jnp.where(t == 0, 0, 100)
    diag_s, chain_s = stencil(
        strip(sigma, rim_sigma),
        lambda row: jnp.where(row < 12, row + 24, row - 16),
        strip_up,
        strip_down,
        (
            lambda row: (row == 8 + bottom) | (row == 16 + top),
            lambda row: (row == 7 + bottom) | (row == 15 + top),
        ),
    )
    del diag, chain
    vectors = []
    rows = []
    d_edge = jnp.concatenate([diag_s[16:24], diag_s[0:8]], axis=0)
    for s in range(2):
        outer = chain_s(strip(xbuf[s], rim[s]), s)
        edge = [jnp.concatenate([v[16:24], v[0:8]], axis=0) for v in outer]
        rows += [a + b for a, b in zip(inner_moments[s], moments(d_edge, *edge))]
        vectors.append(
            [xbuf[s]]
            + [jnp.concatenate([e[0:8], v[8:24], e[8:16]], axis=0) for v, e in zip(inner[s][:3], edge[:3])]
        )

    lane = lax.broadcasted_iota(jnp.int32, (1, LANES), 1)
    low = lane < 64
    surface = []
    for i in range(4):
        both = jnp.where(low, vectors[0][i][:, 0:1], vectors[1][i][:, 0:1])
        surface.append(jnp.sum(jnp.where(here, both, 0.0), axis=0, keepdims=True))

    dots = jnp.sum(jnp.concatenate(rows, axis=0), axis=1, keepdims=True)
    eye = lax.broadcasted_iota(jnp.int32, (12, LANES), 0) == lax.broadcasted_iota(jnp.int32, (12, LANES), 1)
    moment_row = jnp.sum(jnp.where(eye, dots, 0.0), axis=0, keepdims=True)
    packet[...] = jnp.concatenate([moment_row] + surface + [jnp.zeros((3, LANES), jnp.float32)], axis=0)
    pl.semaphore_wait(known.at[1], len(middle))
    copies_t = [
        remote(packet, slots.at[i], tile_send, tile_recv, tile_peer(step)) for i, step in enumerate(STEPS)
    ]
    for copy in copies_t:
        copy.start()
    tell(known.at[2], far)
    every = remote(slots, slots, tile_send, tile_recv, (w, below))
    every.wait_recv()
    total = packet[...] + jnp.sum(slots[...], axis=0)
    pl.semaphore_wait(known.at[2], len(far))

    weight = wt_s[0]
    coefs = []
    for s in range(2):
        nu = [jnp.broadcast_to(total[0:1, 6 * s + m:6 * s + m + 1], (1, LANES)) for m in range(6)]
        mu = [nu[m] - nu[m + 1] for m in range(5)]
        gamma0 = nu[0]
        alpha0 = gamma0 / mu[0]
        za, zb = 1.0 - alpha0, alpha0
        gamma1 = za * za * nu[0] + 2.0 * za * zb * nu[1] + zb * zb * nu[2]
        beta0 = gamma1 / gamma0
        pa, pb = za + beta0, zb
        curve1 = pa * pa * mu[0] + 2.0 * pa * pb * mu[1] + pb * pb * mu[2]
        alpha1 = gamma1 / curve1
        ya, yb, yc = za - alpha1 * pa, zb - alpha1 * (pb - pa), alpha1 * pb
        gamma2 = (
            ya * ya * nu[0] + yb * yb * nu[2] + yc * yc * nu[4]
            + 2.0 * (ya * yb * nu[1] + ya * yc * nu[2] + yb * yc * nu[3])
        )
        beta1 = gamma2 / gamma1
        ra, rb, rc = ya + beta1 * pa, yb + beta1 * pb, yc
        curve2 = (
            ra * ra * mu[0] + rb * rb * mu[2] + rc * rc * mu[4]
            + 2.0 * (ra * rb * mu[1] + ra * rc * mu[2] + rb * rc * mu[3])
        )
        alpha2 = gamma2 / curve2
        coefs.append((
            jnp.full((1, LANES), weight, jnp.float32),
            weight * (alpha0 + alpha1 * pa + alpha2 * ra),
            weight * (alpha1 * pb + alpha2 * rb),
            weight * (alpha2 * rc),
        ))

    low_rows = lax.broadcasted_iota(jnp.int32, (ROWS, LANES), 1) < 64
    for j in range(COLS // LANES):
        part = []
        for s in range(2):
            acc = vectors[s][0][:, j * LANES:(j + 1) * LANES] * coefs[s][0]
            for i in range(1, 4):
                acc = acc + vectors[s][i][:, j * LANES:(j + 1) * LANES] * coefs[s][i]
            part.append(acc)
        chunks[2 * j] = jnp.where(low_rows, part[0], pltpu.roll(part[1], 64, 1))
        chunks[2 * j + 1] = jnp.where(low_rows, pltpu.roll(part[0], 64, 1), part[1])

    copies_first = [
        remote(
            chunks.at[wave_peer(-o)[0]], got_first.at[i], first_send.at[i], first_recv.at[i], wave_peer(c - o)
        )
        for i, (c, o) in enumerate(FIRST_LIST)
    ]
    for copy in copies_first:
        copy.start()

    mine[...] = sum(total[1 + i:2 + i] * jnp.where(low, coefs[0][i], coefs[1][i]) for i in range(4))
    copies_r = [
        remote(mine, slots_r.at[i], r_send, r_recv, wave_peer(i + 1)) for i in range(WAVES - 1)
    ]
    for copy in copies_r:
        copy.start()

    copies_second = []
    for j, c in enumerate(SECOND_LIST):
        acc = chunks[wave_peer(-c)[0]]
        for i, (cc, o) in enumerate(FIRST_LIST):
            if cc == c:
                copies_first[i].wait_recv()
                acc = acc + got_first[i]
        sums[j] = acc
        copy = remote(sums.at[j], got_second.at[j], second_send.at[j], second_recv.at[j], wave_peer(-c))
        copy.start()
        copies_second.append(copy)
    every_r = remote(slots_r, slots_r, r_send, r_recv, wave_peer(1))

    acc = chunks[w]
    for j in reversed(range(len(SECOND_LIST))):
        copies_second[j].wait_recv()
        acc = acc + got_second[j]
    pot[0] = acc[:, :64]
    pot[1] = acc[:, 64:]

    every_r.wait_recv()
    out_r = mine[...] + jnp.sum(slots_r[...], axis=0)
    read[0:1, :] = out_r[:, :64]
    read[1:2, :] = out_r[:, 64:]

    for copy in halos + [every, every_r] + copies_first + copies_second:
        copy.wait_send()


def shards(warm, cls, cond, wn, wt, srow, scol, erow):
    f32 = jnp.float32
    dma = pltpu.SemaphoreType.DMA
    n_first, n_second = len(FIRST_LIST), len(SECOND_LIST)
    return pl.pallas_call(
        kernel,
        out_shape=(
            jax.ShapeDtypeStruct((2, ROWS, COLS // WAVES), f32),
            jax.ShapeDtypeStruct((2, 64), f32),
        ),
        in_specs=[pl.BlockSpec(memory_space=pltpu.HBM)] * 8,
        out_specs=[pl.BlockSpec(memory_space=pltpu.VMEM)] * 2,
        scratch_shapes=[
            pltpu.VMEM((2, ROWS, COLS), f32),
            pltpu.VMEM((ROWS, COLS), jnp.int32),
            pltpu.VMEM((64,), jnp.int32),
            pltpu.SMEM((8,), f32),
            pltpu.SMEM((1,), f32),
            pltpu.SMEM((1,), f32),
            pltpu.SMEM((2,), jnp.int32),
            pltpu.SMEM((2,), jnp.int32),
            pltpu.VMEM((2, 8, COLS + HALF), f32),
            pltpu.VMEM((2, 8, COLS + HALF), f32),
            pltpu.VMEM((8, LANES), f32),
            pltpu.VMEM((TILES - 1, 8, LANES), f32),
            pltpu.VMEM((WAVES, ROWS, LANES), f32),
            pltpu.VMEM((n_first, ROWS, LANES), f32),
            pltpu.VMEM((n_second, ROWS, LANES), f32),
            pltpu.VMEM((n_second, ROWS, LANES), f32),
            pltpu.VMEM((1, LANES), f32),
            pltpu.VMEM((WAVES - 1, 1, LANES), f32),
            dma((8,)),
            dma((2,)), dma((2,)),
            dma, dma,
            dma((n_first,)), dma((n_first,)),
            dma((n_second,)), dma((n_second,)),
            dma, dma,
            pltpu.SemaphoreType.REGULAR((3,)),
        ],
        compiler_params=pltpu.CompilerParams(
            collective_id=0, has_side_effects=True, vmem_limit_bytes=60 * 1024 * 1024
        ),
    )(warm, cls, cond, wn, wt, srow, scol, erow)


def solution(mesh):
    return jax.shard_map(
        shards,
        mesh=mesh,
        in_specs=(
            P("wave", None, "tile", None), P("tile", None), P(), P("wave"), P("wave"), P(), P(), P(),
        ),
        out_specs=(P(None, "tile", "wave"), P()),
        check_vma=False,
    )
```

```python
import jax
import jax.numpy as jnp
from jax import lax
from jax.experimental import pallas as pl
from jax.experimental.pallas import tpu as pltpu
from jax.sharding import PartitionSpec as P

SOURCE_STRENGTH = 50.0
MESH = pl.DeviceIdType.MESH

WAVES = 16
TILES = 32
ROWS = 32
COLS = 1024
LANES = 128

FIRST = {7: (6, 8), -7: (-6,), 4: (3, 5), -4: (-3, -5), 2: (1,), -2: (-1,)}
FIRST_LIST = [(c, o) for c, offsets in FIRST.items() for o in offsets]
SECOND_LIST = list(FIRST)

STEPS = sorted(
    [(a, b, c) for a in range(4) for b in range(4) for c in range(2) if (a, b, c) != (0, 0, 0)],
    key=lambda s: -(min(s[0], 4 - s[0]) + min(s[1], 4 - s[1])),
)
NEAR = [s for s in STEPS if min(s[0], 4 - s[0]) + min(s[1], 4 - s[1]) <= 1]
FAR = [s for s in STEPS if min(s[0], 4 - s[0]) + min(s[1], 4 - s[1]) == 2 and s[2] == 0]


def harmonic(a, b):
    return 2.0 * a * b / (a + b)


def right(v):
    return pltpu.roll(v, COLS - 1, 1)


def left(v):
    return pltpu.roll(v, 1, 1)


def kernel(
    warm, cls, cond, wn, wt, srow, scol, erow,
    pot, read,
    xbuf, cbuf, ebuf, cond_s, wn_s, wt_s, srow_s, scol_s,
    halo_c, halo_x, packet, slots, surfaces, slots_e,
    chunks, got_first, sums, got_second, mine, slots_r,
    in_sem, halo_send, halo_recv, tile_send, tile_recv,
    first_send, first_recv, second_send, second_recv, r_send, r_recv,
    known,
):
    w = lax.axis_index("wave")
    t = lax.axis_index("tile")

    loads = [
        pltpu.make_async_copy(cls, cbuf, in_sem.at[0]),
        pltpu.make_async_copy(cond, cond_s, in_sem.at[1]),
        pltpu.make_async_copy(warm.at[0], xbuf, in_sem.at[2]),
        pltpu.make_async_copy(wn, wn_s, in_sem.at[3]),
        pltpu.make_async_copy(wt, wt_s, in_sem.at[4]),
        pltpu.make_async_copy(srow, srow_s, in_sem.at[5]),
        pltpu.make_async_copy(scol, scol_s, in_sem.at[6]),
        pltpu.make_async_copy(erow, ebuf, in_sem.at[7]),
    ]
    for load in loads:
        load.start()

    below = lax.rem(t + 1, TILES)
    above = lax.rem(t + TILES - 1, TILES)
    t_y, t_x, t_core = t // 8, lax.rem(t // 2, 4), lax.rem(t, 2)

    def tile_peer(step):
        dy, dx, dc = step
        return (w, lax.rem(t_y + dy, 4) * 8 + lax.rem(t_x + dx, 4) * 2 + lax.rem(t_core + dc, 2))

    def wave_peer(k):
        return (lax.rem(w + 2 * WAVES + k, WAVES), t)

    def tell(semaphore, peers):
        for peer in peers:
            pl.semaphore_signal(semaphore, inc=1, device_id=peer, device_id_type=MESH)

    near = [(w, below), (w, above)] + [tile_peer(s) for s in NEAR] + [wave_peer(1), wave_peer(-1)]
    middle = [tile_peer(s) for s in FAR] + [wave_peer(2), wave_peer(-2)]
    far = [wave_peer(4), wave_peer(-4)]
    barrier = pltpu.get_barrier_semaphore()
    tell(barrier, near)

    def remote(src, dst, send, recv, device):
        return pltpu.make_async_remote_copy(
            src_ref=src, dst_ref=dst, send_sem=send, recv_sem=recv, device_id=device, device_id_type=MESH
        )

    first, final = pl.ds(0, 8), pl.ds(ROWS - 8, 8)
    halos = [
        remote(cls.at[first], halo_c.at[0], halo_send.at[0], halo_recv.at[0], (w, above)),
        remote(cls.at[final], halo_c.at[1], halo_send.at[1], halo_recv.at[1], (w, below)),
        remote(warm.at[0, :, first], halo_x.at[0], halo_send.at[2], halo_recv.at[2], (w, above)),
        remote(warm.at[0, :, final], halo_x.at[1], halo_send.at[3], halo_recv.at[3], (w, below)),
    ]
    pl.semaphore_wait(barrier, len(near))
    for copy in halos:
        copy.start()
    tell(known.at[0], near)

    def conductivity(classes):
        value = jnp.full(classes.shape, cond_s[0], jnp.float32)
        for i in range(1, 8):
            value = jnp.where(classes == i, cond_s[i], value)
        return value

    for load in loads:
        load.wait()
    sigma = conductivity(cbuf[...])

    k = wn_s[0]

    def stencil(sig, cell_row, up, down, closed):
        shape = sig.shape
        row = lax.broadcasted_iota(jnp.int32, shape, 0)
        col = lax.broadcasted_iota(jnp.int32, shape, 1)
        last = col == COLS - 1
        face_down = harmonic(sig, down(sig, 0))
        if closed is None:
            face_up = up(face_down, None)
        else:
            face_up = jnp.where(row == closed[0], 0.0, harmonic(sig, up(sig, 0)))
            face_down = jnp.where(row == closed[1], 0.0, face_down)
        face_right = jnp.where(last, 0.0, harmonic(sig, right(sig)))
        face_left = left(face_right)
        diag = face_up + face_down + face_left + face_right + jnp.where(last, sig, 0.0) + (k * k) * sig
        inv = 1.0 / diag
        a_up, a_down, a_left, a_right = face_up * inv, face_down * inv, face_left * inv, face_right * inv

        def apply(v, tag):
            return a_up * up(v, tag) + a_down * down(v, tag) + a_left * left(v) + a_right * right(v)

        def chain(x, s):
            q = jnp.where((cell_row(row) + t * ROWS == srow_s[s]) & (col == scol_s[s]), SOURCE_STRENGTH, 0.0)
            v0 = q * inv - x + apply(x, (s, 0))
            v1 = apply(v0, (s, 1))
            v2 = apply(v1, (s, 2))
            return v0, v1, v2, apply(v2, (s, 3))

        return diag, chain

    def fold(product):
        total = product[:, :LANES]
        for j in range(1, COLS // LANES):
            total = total + product[:, j * LANES:(j + 1) * LANES]
        return total

    def moments(d, v0, v1, v2, v3):
        d0, d1, d2 = d * v0, d * v1, d * v2
        return [fold(a * b) for a, b in ((d0, v0), (d0, v1), (d1, v1), (d1, v2), (d2, v2), (d2, v3))]

    sub = lax.broadcasted_iota(jnp.int32, (8, COLS), 0)
    upper = sub < 4
    upper_lanes = lax.broadcasted_iota(jnp.int32, (8, LANES), 0) < 4

    diag, chain = stencil(
        sigma,
        lambda row: row,
        lambda v, tag: pltpu.roll(v, 1, 0),
        lambda v, tag: pltpu.roll(v, ROWS - 1, 0),
        None,
    )
    inner = [chain(xbuf[s], s) for s in range(2)]
    inner_moments = [
        [f[8:16] + f[16:24] + jnp.where(upper_lanes, f[24:32], f[0:8]) for f in moments(diag, *inner[s])]
        for s in range(2)
    ]
    own = {0: (sigma[0:8], sigma[24:32])}
    for s in range(2):
        own[(s, 0)] = (xbuf[s, 0:8, :], xbuf[s, 24:32, :])
        for i in range(3):
            own[(s, i + 1)] = (inner[s][i][0:8], inner[s][i][24:32])

    electrode = ebuf[...].reshape(1, 64)
    electrode = jnp.concatenate([electrode, electrode], axis=1)
    here = lax.broadcasted_iota(jnp.int32, (ROWS, LANES), 0) + t * ROWS == electrode

    for copy in halos:
        copy.wait_recv()
    pl.semaphore_wait(known.at[0], len(near))
    tell(known.at[1], middle)

    edge_stencil = [
        stencil(
            jnp.where(upper, sigma[0:8], conductivity(halo_c[1])),
            lambda row: jnp.where(row < 4, row, row - 8),
            lambda v, tag: pltpu.roll(v, 1, 0),
            lambda v, tag: pltpu.roll(jnp.where(sub == 4, own[tag][0], v), 7, 0),
            (jnp.where(t == 0, 0, -1), jnp.where(t == 0, 7, -1)),
        ),
        stencil(
            jnp.where(upper, conductivity(halo_c[0]), sigma[24:32]),
            lambda row: jnp.where(row < 4, row + 32, row + 24),
            lambda v, tag: pltpu.roll(jnp.where(sub == 3, own[tag][1], v), 1, 0),
            lambda v, tag: pltpu.roll(v, 7, 0),
            (jnp.where(t == TILES - 1, 0, -1), jnp.where(t == TILES - 1, 7, -1)),
        ),
    ]
    edges = []
    rows = []
    for s in range(2):
        block0 = edge_stencil[0][1](jnp.where(upper, own[(s, 0)][0], halo_x[1, s]), s)
        block1 = edge_stencil[1][1](jnp.where(upper, halo_x[0, s], own[(s, 0)][1]), s)
        outer = zip(moments(edge_stencil[0][0], *block0), moments(edge_stencil[1][0], *block1))
        rows += [
            jnp.sum(a + jnp.where(upper_lanes, b, c), axis=0, keepdims=True)
            for a, (b, c) in zip(inner_moments[s], outer)
        ]
        edges.append((block0, block1))

    dots = jnp.sum(jnp.concatenate(rows, axis=0), axis=1, keepdims=True)
    eye = lax.broadcasted_iota(jnp.int32, (12, LANES), 0) == lax.broadcasted_iota(jnp.int32, (12, LANES), 1)
    packet[...] = jnp.sum(jnp.where(eye, dots, 0.0), axis=0, keepdims=True)
    pl.semaphore_wait(known.at[1], len(middle))
    peers = [tile_peer(step) for step in STEPS]
    for i, peer in enumerate(peers):
        remote(packet, slots.at[i], tile_send.at[0], tile_recv.at[0], peer).start()
    tell(known.at[2], far)

    vectors = [
        [xbuf[s]]
        + [
            jnp.concatenate(
                [
                    jnp.where(upper, edges[s][0][i], inner[s][i][0:8]),
                    inner[s][i][8:24],
                    jnp.where(upper, inner[s][i][24:32], edges[s][1][i]),
                ],
                axis=0,
            )
            for i in range(3)
        ]
        for s in range(2)
    ]
    lane = lax.broadcasted_iota(jnp.int32, (1, LANES), 1)
    low = lane < 64
    surface = []
    for i in range(4):
        both = jnp.where(low, vectors[0][i][:, 0:1], vectors[1][i][:, 0:1])
        surface.append(jnp.sum(jnp.where(here, both, 0.0), axis=0, keepdims=True))
    surfaces[...] = jnp.concatenate(surface, axis=0)
    for i, peer in enumerate(peers):
        remote(surfaces, slots_e.at[i], tile_send.at[1], tile_recv.at[1], peer).start()

    every = remote(slots, slots, tile_send.at[0], tile_recv.at[0], (w, below))
    every_e = remote(slots_e, slots_e, tile_send.at[1], tile_recv.at[1], (w, below))
    every.wait_recv()
    total = packet[...] + jnp.sum(slots[...], axis=0)
    pl.semaphore_wait(known.at[2], len(far))

    weight = wt_s[0]
    coefs = []
    for s in range(2):
        nu = [jnp.broadcast_to(total[0:1, 6 * s + m:6 * s + m + 1], (1, LANES)) for m in range(6)]
        mu = [nu[m] - nu[m + 1] for m in range(5)]
        gamma0 = nu[0]
        alpha0 = gamma0 / mu[0]
        za, zb = 1.0 - alpha0, alpha0
        gamma1 = za * za * nu[0] + 2.0 * za * zb * nu[1] + zb * zb * nu[2]
        beta0 = gamma1 / gamma0
        pa, pb = za + beta0, zb
        curve1 = pa * pa * mu[0] + 2.0 * pa * pb * mu[1] + pb * pb * mu[2]
        alpha1 = gamma1 / curve1
        ya, yb, yc = za - alpha1 * pa, zb - alpha1 * (pb - pa), alpha1 * pb
        gamma2 = (
            ya * ya * nu[0] + yb * yb * nu[2] + yc * yc * nu[4]
            + 2.0 * (ya * yb * nu[1] + ya * yc * nu[2] + yb * yc * nu[3])
        )
        beta1 = gamma2 / gamma1
        ra, rb, rc = ya + beta1 * pa, yb + beta1 * pb, yc
        curve2 = (
            ra * ra * mu[0] + rb * rb * mu[2] + rc * rc * mu[4]
            + 2.0 * (ra * rb * mu[1] + ra * rc * mu[2] + rb * rc * mu[3])
        )
        alpha2 = gamma2 / curve2
        coefs.append((
            jnp.full((1, LANES), weight, jnp.float32),
            weight * (alpha0 + alpha1 * pa + alpha2 * ra),
            weight * (alpha1 * pb + alpha2 * rb),
            weight * (alpha2 * rc),
        ))

    low_rows = lax.broadcasted_iota(jnp.int32, (ROWS, LANES), 1) < 64
    for j in range(COLS // LANES):
        part = []
        for s in range(2):
            acc = vectors[s][0][:, j * LANES:(j + 1) * LANES] * coefs[s][0]
            for i in range(1, 4):
                acc = acc + vectors[s][i][:, j * LANES:(j + 1) * LANES] * coefs[s][i]
            part.append(acc)
        chunks[2 * j] = jnp.where(low_rows, part[0], pltpu.roll(part[1], 64, 1))
        chunks[2 * j + 1] = jnp.where(low_rows, pltpu.roll(part[0], 64, 1), part[1])

    copies_first = [
        remote(
            chunks.at[wave_peer(-o)[0]], got_first.at[i], first_send.at[i], first_recv.at[i], wave_peer(c - o)
        )
        for i, (c, o) in enumerate(FIRST_LIST)
    ]
    for copy in copies_first:
        copy.start()

    every_e.wait_recv()
    total_e = surfaces[...] + jnp.sum(slots_e[...], axis=0)
    mine[...] = sum(total_e[i:i + 1] * jnp.where(low, coefs[0][i], coefs[1][i]) for i in range(4))
    copies_r = [
        remote(mine, slots_r.at[i], r_send, r_recv, wave_peer(i + 1)) for i in range(WAVES - 1)
    ]
    for copy in copies_r:
        copy.start()

    copies_second = []
    for j, c in enumerate(SECOND_LIST):
        acc = chunks[wave_peer(-c)[0]]
        for i, (cc, o) in enumerate(FIRST_LIST):
            if cc == c:
                copies_first[i].wait_recv()
                acc = acc + got_first[i]
        sums[j] = acc
        copy = remote(sums.at[j], got_second.at[j], second_send.at[j], second_recv.at[j], wave_peer(-c))
        copy.start()
        copies_second.append(copy)
    every_r = remote(slots_r, slots_r, r_send, r_recv, wave_peer(1))

    acc = chunks[w]
    for j in reversed(range(len(SECOND_LIST))):
        copies_second[j].wait_recv()
        acc = acc + got_second[j]
    pot[0] = acc[:, :64]
    pot[1] = acc[:, 64:]

    every_r.wait_recv()
    out_r = mine[...] + jnp.sum(slots_r[...], axis=0)
    read[0:1, :] = out_r[:, :64]
    read[1:2, :] = out_r[:, 64:]

    for copy in halos + [every, every_e, every_r] + copies_first + copies_second:
        copy.wait_send()


def shards(warm, cls, cond, wn, wt, srow, scol, erow):
    f32 = jnp.float32
    dma = pltpu.SemaphoreType.DMA
    n_first, n_second = len(FIRST_LIST), len(SECOND_LIST)
    return pl.pallas_call(
        kernel,
        out_shape=(
            jax.ShapeDtypeStruct((2, ROWS, COLS // WAVES), f32),
            jax.ShapeDtypeStruct((2, 64), f32),
        ),
        in_specs=[pl.BlockSpec(memory_space=pltpu.HBM)] * 8,
        out_specs=[pl.BlockSpec(memory_space=pltpu.VMEM)] * 2,
        scratch_shapes=[
            pltpu.VMEM((2, ROWS, COLS), f32),
            pltpu.VMEM((ROWS, COLS), jnp.int32),
            pltpu.VMEM((64,), jnp.int32),
            pltpu.SMEM((8,), f32),
            pltpu.SMEM((1,), f32),
            pltpu.SMEM((1,), f32),
            pltpu.SMEM((2,), jnp.int32),
            pltpu.SMEM((2,), jnp.int32),
            pltpu.VMEM((2, 8, COLS), jnp.int32),
            pltpu.VMEM((2, 2, 8, COLS), f32),
            pltpu.VMEM((1, LANES), f32),
            pltpu.VMEM((TILES - 1, 1, LANES), f32),
            pltpu.VMEM((4, LANES), f32),
            pltpu.VMEM((TILES - 1, 4, LANES), f32),
            pltpu.VMEM((WAVES, ROWS, LANES), f32),
            pltpu.VMEM((n_first, ROWS, LANES), f32),
            pltpu.VMEM((n_second, ROWS, LANES), f32),
            pltpu.VMEM((n_second, ROWS, LANES), f32),
            pltpu.VMEM((1, LANES), f32),
            pltpu.VMEM((WAVES - 1, 1, LANES), f32),
            dma((8,)),
            dma((4,)), dma((4,)),
            dma((2,)), dma((2,)),
            dma((n_first,)), dma((n_first,)),
            dma((n_second,)), dma((n_second,)),
            dma, dma,
            pltpu.SemaphoreType.REGULAR((3,)),
        ],
        compiler_params=pltpu.CompilerParams(
            collective_id=0, has_side_effects=True, vmem_limit_bytes=55168 * 1024
        ),
    )(warm, cls, cond, wn, wt, srow, scol, erow)


def solution(mesh):
    return jax.shard_map(
        shards,
        mesh=mesh,
        in_specs=(
            P("wave", None, "tile", None), P("tile", None), P(), P("wave"), P("wave"), P(), P(), P(),
        ),
        out_specs=(P(None, "tile", "wave"), P()),
        check_vma=False,
    )
```

```python
import jax
import jax.numpy as jnp
from jax import lax
from jax.experimental import pallas as pl
from jax.experimental.pallas import tpu as pltpu
from jax.sharding import PartitionSpec as P

SOURCE_STRENGTH = 50.0
MESH = pl.DeviceIdType.MESH

WAVES = 16
TILES = 32
ROWS = 32
COLS = 1024
LANES = 128

FIRST = {7: (6, 8), -7: (-6,), 4: (3, 5), -4: (-3, -5), 2: (1,), -2: (-1,)}
FIRST_LIST = [(c, o) for c, offsets in FIRST.items() for o in offsets]
SECOND_LIST = list(FIRST)

STEPS = sorted(
    [(a, b, c) for a in range(4) for b in range(4) for c in range(2) if (a, b, c) != (0, 0, 0)],
    key=lambda s: -(min(s[0], 4 - s[0]) + min(s[1], 4 - s[1])),
)
NEAR = [s for s in STEPS if min(s[0], 4 - s[0]) + min(s[1], 4 - s[1]) <= 1]
FAR = [s for s in STEPS if min(s[0], 4 - s[0]) + min(s[1], 4 - s[1]) == 2 and s[2] == 0]


def harmonic(a, b):
    return 2.0 * a * b / (a + b)


def right(v):
    return pltpu.roll(v, COLS - 1, 1)


def left(v):
    return pltpu.roll(v, 1, 1)


def kernel(
    warm, cls, cond, wn, wt, srow, scol, erow,
    pot, read,
    xbuf, cbuf, ebuf, cond_s, wn_s, wt_s, srow_s, scol_s,
    halo_c, halo_x, packet, slots, surfaces, slots_e,
    chunks, got_first, sums, got_second, mine, slots_r,
    in_sem, halo_send, halo_recv, tile_send, tile_recv,
    first_send, first_recv, second_send, second_recv, r_send, r_recv,
    known,
):
    w = lax.axis_index("wave")
    t = lax.axis_index("tile")

    loads = [
        pltpu.make_async_copy(cls, cbuf, in_sem.at[0]),
        pltpu.make_async_copy(cond, cond_s, in_sem.at[1]),
        pltpu.make_async_copy(warm.at[0], xbuf, in_sem.at[2]),
        pltpu.make_async_copy(wn, wn_s, in_sem.at[3]),
        pltpu.make_async_copy(wt, wt_s, in_sem.at[4]),
        pltpu.make_async_copy(srow, srow_s, in_sem.at[5]),
        pltpu.make_async_copy(scol, scol_s, in_sem.at[6]),
        pltpu.make_async_copy(erow, ebuf, in_sem.at[7]),
    ]
    for load in loads:
        load.start()

    below = lax.rem(t + 1, TILES)
    above = lax.rem(t + TILES - 1, TILES)
    t_y, t_x, t_core = t // 8, lax.rem(t // 2, 4), lax.rem(t, 2)

    def tile_peer(step):
        dy, dx, dc = step
        return (w, lax.rem(t_y + dy, 4) * 8 + lax.rem(t_x + dx, 4) * 2 + lax.rem(t_core + dc, 2))

    def wave_peer(k):
        return (lax.rem(w + 2 * WAVES + k, WAVES), t)

    def tell(semaphore, peers):
        for peer in peers:
            pl.semaphore_signal(semaphore, inc=1, device_id=peer, device_id_type=MESH)

    near = [(w, below), (w, above)] + [tile_peer(s) for s in NEAR] + [wave_peer(1), wave_peer(-1)]
    middle = [tile_peer(s) for s in FAR] + [wave_peer(2), wave_peer(-2)]
    far = [wave_peer(4), wave_peer(-4)]
    barrier = pltpu.get_barrier_semaphore()
    tell(barrier, near)

    def remote(src, dst, send, recv, device):
        return pltpu.make_async_remote_copy(
            src_ref=src, dst_ref=dst, send_sem=send, recv_sem=recv, device_id=device, device_id_type=MESH
        )

    first, final = pl.ds(0, 8), pl.ds(ROWS - 8, 8)
    halos = [
        remote(cls.at[first], halo_c.at[0], halo_send.at[0], halo_recv.at[0], (w, above)),
        remote(cls.at[final], halo_c.at[1], halo_send.at[1], halo_recv.at[1], (w, below)),
        remote(warm.at[0, :, first], halo_x.at[0], halo_send.at[2], halo_recv.at[2], (w, above)),
        remote(warm.at[0, :, final], halo_x.at[1], halo_send.at[3], halo_recv.at[3], (w, below)),
    ]
    pl.semaphore_wait(barrier, len(near))
    for copy in halos:
        copy.start()
    tell(known.at[0], near)

    def conductivity(classes):
        value = jnp.full(classes.shape, cond_s[0], jnp.float32)
        for i in range(1, 8):
            value = jnp.where(classes == i, cond_s[i], value)
        return value

    for load in loads:
        load.wait()
    sigma = conductivity(cbuf[...])
    pl.semaphore_wait(known.at[0], len(near))
    tell(known.at[1], middle)

    k = wn_s[0]

    def stencil(sig, cell_row, up, down, closed):
        shape = sig.shape
        row = lax.broadcasted_iota(jnp.int32, shape, 0)
        col = lax.broadcasted_iota(jnp.int32, shape, 1)
        last = col == COLS - 1
        face_down = harmonic(sig, down(sig, 0))
        if closed is None:
            face_up = up(face_down, None)
        else:
            face_up = jnp.where(row == closed[0], 0.0, harmonic(sig, up(sig, 0)))
            face_down = jnp.where(row == closed[1], 0.0, face_down)
        face_right = jnp.where(last, 0.0, harmonic(sig, right(sig)))
        face_left = left(face_right)
        diag = face_up + face_down + face_left + face_right + jnp.where(last, sig, 0.0) + (k * k) * sig
        inv = 1.0 / diag
        a_up, a_down, a_left, a_right = face_up * inv, face_down * inv, face_left * inv, face_right * inv

        def apply(v, tag):
            return a_up * up(v, tag) + a_down * down(v, tag) + a_left * left(v) + a_right * right(v)

        def begin(x, s):
            q = jnp.where((cell_row(row) + t * ROWS == srow_s[s]) & (col == scol_s[s]), SOURCE_STRENGTH, 0.0)
            return q * inv - x + apply(x, (s, 0))

        return diag, begin, apply

    def chains(work):
        v0 = [st[1](x, s) for st, x, s in work]
        v1 = [st[2](v, (s, 1)) for (st, _, s), v in zip(work, v0)]
        v2 = [st[2](v, (s, 2)) for (st, _, s), v in zip(work, v1)]
        v3 = [st[2](v, (s, 3)) for (st, _, s), v in zip(work, v2)]
        return list(zip(v0, v1, v2, v3))

    def fold(product):
        total = product[:, :LANES]
        for j in range(1, COLS // LANES):
            total = total + product[:, j * LANES:(j + 1) * LANES]
        return total

    def moments(d, v0, v1, v2, v3):
        d0, d1, d2 = d * v0, d * v1, d * v2
        return [fold(a * b) for a, b in ((d0, v0), (d0, v1), (d1, v1), (d1, v2), (d2, v2), (d2, v3))]

    sub = lax.broadcasted_iota(jnp.int32, (8, COLS), 0)
    upper = sub < 4
    upper_lanes = lax.broadcasted_iota(jnp.int32, (8, LANES), 0) < 4

    whole = stencil(
        sigma,
        lambda row: row,
        lambda v, tag: pltpu.roll(v, 1, 0),
        lambda v, tag: pltpu.roll(v, ROWS - 1, 0),
        None,
    )
    inner = chains([(whole, xbuf[s], s) for s in range(2)])
    inner_moments = [
        [f[8:16] + f[16:24] + jnp.where(upper_lanes, f[24:32], f[0:8]) for f in moments(whole[0], *inner[s])]
        for s in range(2)
    ]
    own = {0: (sigma[0:8], sigma[24:32])}
    for s in range(2):
        own[(s, 0)] = (xbuf[s, 0:8, :], xbuf[s, 24:32, :])
        for i in range(3):
            own[(s, i + 1)] = (inner[s][i][0:8], inner[s][i][24:32])

    electrode = ebuf[...].reshape(1, 64)
    electrode = jnp.concatenate([electrode, electrode], axis=1)
    here = lax.broadcasted_iota(jnp.int32, (ROWS, LANES), 0) + t * ROWS == electrode

    for copy in halos:
        copy.wait_recv()
    pl.semaphore_wait(known.at[1], len(middle))
    tell(known.at[2], far)

    edge_stencil = [
        stencil(
            jnp.where(upper, sigma[0:8], conductivity(halo_c[1])),
            lambda row: jnp.where(row < 4, row, row - 8),
            lambda v, tag: pltpu.roll(v, 1, 0),
            lambda v, tag: pltpu.roll(jnp.where(sub == 4, own[tag][0], v), 7, 0),
            (jnp.where(t == 0, 0, -1), jnp.where(t == 0, 7, -1)),
        ),
        stencil(
            jnp.where(upper, conductivity(halo_c[0]), sigma[24:32]),
            lambda row: jnp.where(row < 4, row + 32, row + 24),
            lambda v, tag: pltpu.roll(jnp.where(sub == 3, own[tag][1], v), 1, 0),
            lambda v, tag: pltpu.roll(v, 7, 0),
            (jnp.where(t == TILES - 1, 0, -1), jnp.where(t == TILES - 1, 7, -1)),
        ),
    ]
    outer = chains(
        [(edge_stencil[0], jnp.where(upper, own[(s, 0)][0], halo_x[1, s]), s) for s in range(2)]
        + [(edge_stencil[1], jnp.where(upper, halo_x[0, s], own[(s, 0)][1]), s) for s in range(2)]
    )
    edges = [(outer[s], outer[2 + s]) for s in range(2)]
    rows = []
    for s in range(2):
        pairs = zip(moments(edge_stencil[0][0], *edges[s][0]), moments(edge_stencil[1][0], *edges[s][1]))
        rows += [
            jnp.sum(a + jnp.where(upper_lanes, b, c), axis=0, keepdims=True)
            for a, (b, c) in zip(inner_moments[s], pairs)
        ]

    dots = jnp.sum(jnp.concatenate(rows, axis=0), axis=1, keepdims=True)
    eye = lax.broadcasted_iota(jnp.int32, (12, LANES), 0) == lax.broadcasted_iota(jnp.int32, (12, LANES), 1)
    packet[...] = jnp.sum(jnp.where(eye, dots, 0.0), axis=0, keepdims=True)
    peers = [tile_peer(step) for step in STEPS]
    for i, peer in enumerate(peers):
        remote(packet, slots.at[i], tile_send.at[0], tile_recv.at[0], peer).start()

    vectors = [
        [xbuf[s]]
        + [
            jnp.concatenate(
                [
                    jnp.where(upper, edges[s][0][i], inner[s][i][0:8]),
                    inner[s][i][8:24],
                    jnp.where(upper, inner[s][i][24:32], edges[s][1][i]),
                ],
                axis=0,
            )
            for i in range(3)
        ]
        for s in range(2)
    ]
    lane = lax.broadcasted_iota(jnp.int32, (1, LANES), 1)
    low = lane < 64
    surface = []
    for i in range(4):
        both = jnp.where(low, vectors[0][i][:, 0:1], vectors[1][i][:, 0:1])
        surface.append(jnp.sum(jnp.where(here, both, 0.0), axis=0, keepdims=True))
    surfaces[...] = jnp.concatenate(surface, axis=0)
    for i, peer in enumerate(peers):
        remote(surfaces, slots_e.at[i], tile_send.at[1], tile_recv.at[1], peer).start()

    every = remote(slots, slots, tile_send.at[0], tile_recv.at[0], (w, below))
    every_e = remote(slots_e, slots_e, tile_send.at[1], tile_recv.at[1], (w, below))
    every.wait_recv()
    total = packet[...] + jnp.sum(slots[...], axis=0)
    pl.semaphore_wait(known.at[2], len(far))

    weight = wt_s[0]
    coefs = []
    for s in range(2):
        nu = [jnp.broadcast_to(total[0:1, 6 * s + m:6 * s + m + 1], (1, LANES)) for m in range(6)]
        mu = [nu[m] - nu[m + 1] for m in range(5)]
        gamma0 = nu[0]
        alpha0 = gamma0 / mu[0]
        za, zb = 1.0 - alpha0, alpha0
        gamma1 = za * za * nu[0] + 2.0 * za * zb * nu[1] + zb * zb * nu[2]
        beta0 = gamma1 / gamma0
        pa, pb = za + beta0, zb
        curve1 = pa * pa * mu[0] + 2.0 * pa * pb * mu[1] + pb * pb * mu[2]
        alpha1 = gamma1 / curve1
        ya, yb, yc = za - alpha1 * pa, zb - alpha1 * (pb - pa), alpha1 * pb
        gamma2 = (
            ya * ya * nu[0] + yb * yb * nu[2] + yc * yc * nu[4]
            + 2.0 * (ya * yb * nu[1] + ya * yc * nu[2] + yb * yc * nu[3])
        )
        beta1 = gamma2 / gamma1
        ra, rb, rc = ya + beta1 * pa, yb + beta1 * pb, yc
        curve2 = (
            ra * ra * mu[0] + rb * rb * mu[2] + rc * rc * mu[4]
            + 2.0 * (ra * rb * mu[1] + ra * rc * mu[2] + rb * rc * mu[3])
        )
        alpha2 = gamma2 / curve2
        coefs.append((
            jnp.full((1, LANES), weight, jnp.float32),
            weight * (alpha0 + alpha1 * pa + alpha2 * ra),
            weight * (alpha1 * pb + alpha2 * rb),
            weight * (alpha2 * rc),
        ))

    low_rows = lax.broadcasted_iota(jnp.int32, (ROWS, LANES), 1) < 64
    for j in range(COLS // LANES):
        part = []
        for s in range(2):
            acc = vectors[s][0][:, j * LANES:(j + 1) * LANES] * coefs[s][0]
            for i in range(1, 4):
                acc = acc + vectors[s][i][:, j * LANES:(j + 1) * LANES] * coefs[s][i]
            part.append(acc)
        chunks[2 * j] = jnp.where(low_rows, part[0], pltpu.roll(part[1], 64, 1))
        chunks[2 * j + 1] = jnp.where(low_rows, pltpu.roll(part[0], 64, 1), part[1])

    copies_first = [
        remote(
            chunks.at[wave_peer(-o)[0]], got_first.at[i], first_send.at[i], first_recv.at[i], wave_peer(c - o)
        )
        for i, (c, o) in enumerate(FIRST_LIST)
    ]
    for copy in copies_first:
        copy.start()

    every_e.wait_recv()
    total_e = surfaces[...] + jnp.sum(slots_e[...], axis=0)
    mine[...] = sum(total_e[i:i + 1] * jnp.where(low, coefs[0][i], coefs[1][i]) for i in range(4))
    copies_r = [
        remote(mine, slots_r.at[i], r_send, r_recv, wave_peer(i + 1)) for i in range(WAVES - 1)
    ]
    for copy in copies_r:
        copy.start()

    copies_second = []
    for j, c in enumerate(SECOND_LIST):
        acc = chunks[wave_peer(-c)[0]]
        for i, (cc, o) in enumerate(FIRST_LIST):
            if cc == c:
                copies_first[i].wait_recv()
                acc = acc + got_first[i]
        sums[j] = acc
        copy = remote(sums.at[j], got_second.at[j], second_send.at[j], second_recv.at[j], wave_peer(-c))
        copy.start()
        copies_second.append(copy)
    every_r = remote(slots_r, slots_r, r_send, r_recv, wave_peer(1))

    acc = chunks[w]
    for j in reversed(range(len(SECOND_LIST))):
        copies_second[j].wait_recv()
        acc = acc + got_second[j]
    pot[0] = acc[:, :64]
    pot[1] = acc[:, 64:]

    every_r.wait_recv()
    out_r = mine[...] + jnp.sum(slots_r[...], axis=0)
    read[0:1, :] = out_r[:, :64]
    read[1:2, :] = out_r[:, 64:]

    for copy in halos + [every, every_e, every_r] + copies_first + copies_second:
        copy.wait_send()


def shards(warm, cls, cond, wn, wt, srow, scol, erow):
    f32 = jnp.float32
    dma = pltpu.SemaphoreType.DMA
    n_first, n_second = len(FIRST_LIST), len(SECOND_LIST)
    return pl.pallas_call(
        kernel,
        out_shape=(
            jax.ShapeDtypeStruct((2, ROWS, COLS // WAVES), f32),
            jax.ShapeDtypeStruct((2, 64), f32),
        ),
        in_specs=[pl.BlockSpec(memory_space=pltpu.HBM)] * 8,
        out_specs=[pl.BlockSpec(memory_space=pltpu.VMEM)] * 2,
        scratch_shapes=[
            pltpu.VMEM((2, ROWS, COLS), f32),
            pltpu.VMEM((ROWS, COLS), jnp.int32),
            pltpu.VMEM((64,), jnp.int32),
            pltpu.SMEM((8,), f32),
            pltpu.SMEM((1,), f32),
            pltpu.SMEM((1,), f32),
            pltpu.SMEM((2,), jnp.int32),
            pltpu.SMEM((2,), jnp.int32),
            pltpu.VMEM((2, 8, COLS), jnp.int32),
            pltpu.VMEM((2, 2, 8, COLS), f32),
            pltpu.VMEM((1, LANES), f32),
            pltpu.VMEM((TILES - 1, 1, LANES), f32),
            pltpu.VMEM((4, LANES), f32),
            pltpu.VMEM((TILES - 1, 4, LANES), f32),
            pltpu.VMEM((WAVES, ROWS, LANES), f32),
            pltpu.VMEM((n_first, ROWS, LANES), f32),
            pltpu.VMEM((n_second, ROWS, LANES), f32),
            pltpu.VMEM((n_second, ROWS, LANES), f32),
            pltpu.VMEM((1, LANES), f32),
            pltpu.VMEM((WAVES - 1, 1, LANES), f32),
            dma((8,)),
            dma((4,)), dma((4,)),
            dma((2,)), dma((2,)),
            dma((n_first,)), dma((n_first,)),
            dma((n_second,)), dma((n_second,)),
            dma, dma,
            pltpu.SemaphoreType.REGULAR((3,)),
        ],
        compiler_params=pltpu.CompilerParams(
            collective_id=0, has_side_effects=True, vmem_limit_bytes=55168 * 1024
        ),
    )(warm, cls, cond, wn, wt, srow, scol, erow)


def solution(mesh):
    return jax.shard_map(
        shards,
        mesh=mesh,
        in_specs=(
            P("wave", None, "tile", None), P("tile", None), P(), P("wave"), P("wave"), P(), P(), P(),
        ),
        out_specs=(P(None, "tile", "wave"), P()),
        check_vma=False,
    )
```

```python
import jax
import jax.numpy as jnp
from jax import lax
from jax.experimental import pallas as pl
from jax.experimental.pallas import tpu as pltpu
from jax.sharding import PartitionSpec as P

SOURCE_STRENGTH = 50.0
N_FAR_R = 7
MESH = pl.DeviceIdType.MESH

WAVES = 16
TILES = 32
ROWS = 32
COLS = 1024
LANES = 128

FIRST = {6: (8, 7, 5), -6: (-7, -5), 3: (4, 2), -3: (-4, -2), 0: (1, -1)}
FIRST_LIST = [(c, o) for c, offsets in FIRST.items() for o in offsets]
SECOND_LIST = [c for c in FIRST if c != 0]

STEPS = sorted(
    [(a, b, c) for a in range(4) for b in range(4) for c in range(2) if (a, b, c) != (0, 0, 0)],
    key=lambda s: -(min(s[0], 4 - s[0]) + min(s[1], 4 - s[1])),
)
NEAR = [s for s in STEPS if min(s[0], 4 - s[0]) + min(s[1], 4 - s[1]) <= 1]
FAR = [s for s in STEPS if min(s[0], 4 - s[0]) + min(s[1], 4 - s[1]) == 2 and s[2] == 0]


def harmonic(a, b):
    return 2.0 * a * b / (a + b)


def right(v):
    return pltpu.roll(v, COLS - 1, 1)


def left(v):
    return pltpu.roll(v, 1, 1)


def kernel(
    warm, cls, cond, wn, wt, srow, scol, erow,
    pot, read,
    xbuf, cbuf, ebuf, cond_s, wn_s, wt_s, srow_s, scol_s,
    halo_c, halo_x, packet, slots, surfaces, slots_e,
    chunks, got_first, sums, got_second, mine, slots_r,
    in_sem, halo_send, halo_recv, tile_send, tile_recv,
    first_send, first_recv, second_send, second_recv, r_send, r_recv,
    known,
):
    w = lax.axis_index("wave")
    t = lax.axis_index("tile")

    loads = [
        pltpu.make_async_copy(cls, cbuf, in_sem.at[0]),
        pltpu.make_async_copy(cond, cond_s, in_sem.at[1]),
        pltpu.make_async_copy(warm.at[0], xbuf, in_sem.at[2]),
        pltpu.make_async_copy(wn, wn_s, in_sem.at[3]),
        pltpu.make_async_copy(wt, wt_s, in_sem.at[4]),
        pltpu.make_async_copy(srow, srow_s, in_sem.at[5]),
        pltpu.make_async_copy(scol, scol_s, in_sem.at[6]),
        pltpu.make_async_copy(erow, ebuf, in_sem.at[7]),
    ]
    for load in loads:
        load.start()

    below = lax.rem(t + 1, TILES)
    above = lax.rem(t + TILES - 1, TILES)
    t_y, t_x, t_core = t // 8, lax.rem(t // 2, 4), lax.rem(t, 2)

    def tile_peer(step):
        dy, dx, dc = step
        return (w, lax.rem(t_y + dy, 4) * 8 + lax.rem(t_x + dx, 4) * 2 + lax.rem(t_core + dc, 2))

    def wave_peer(k):
        return (lax.rem(w + 2 * WAVES + k, WAVES), t)

    def tell(semaphore, peers):
        for peer in peers:
            pl.semaphore_signal(semaphore, inc=1, device_id=peer, device_id_type=MESH)

    near = [(w, below), (w, above)] + [tile_peer(s) for s in NEAR] + [wave_peer(1), wave_peer(-1)]
    middle = [tile_peer(s) for s in FAR] + [wave_peer(2), wave_peer(-2)]
    far = [wave_peer(4), wave_peer(-4)]
    barrier = pltpu.get_barrier_semaphore()
    tell(barrier, near)

    def remote(src, dst, send, recv, device):
        return pltpu.make_async_remote_copy(
            src_ref=src, dst_ref=dst, send_sem=send, recv_sem=recv, device_id=device, device_id_type=MESH
        )

    first, final = pl.ds(0, 8), pl.ds(ROWS - 8, 8)
    halos = [
        remote(cls.at[first], halo_c.at[0], halo_send.at[0], halo_recv.at[0], (w, above)),
        remote(cls.at[final], halo_c.at[1], halo_send.at[1], halo_recv.at[1], (w, below)),
        remote(warm.at[0, :, first], halo_x.at[0], halo_send.at[2], halo_recv.at[2], (w, above)),
        remote(warm.at[0, :, final], halo_x.at[1], halo_send.at[3], halo_recv.at[3], (w, below)),
    ]
    pl.semaphore_wait(barrier, len(near))
    for copy in halos:
        copy.start()
    tell(known.at[0], near)

    def conductivity(classes):
        value = jnp.full(classes.shape, cond_s[0], jnp.float32)
        for i in range(1, 8):
            value = jnp.where(classes == i, cond_s[i], value)
        return value

    for load in loads:
        load.wait()
    sigma = conductivity(cbuf[...])
    pl.semaphore_wait(known.at[0], len(near))
    tell(known.at[1], middle)

    k = wn_s[0]

    def stencil(sig, cell_row, up, down, closed):
        shape = sig.shape
        row = lax.broadcasted_iota(jnp.int32, shape, 0)
        col = lax.broadcasted_iota(jnp.int32, shape, 1)
        last = col == COLS - 1
        face_down = harmonic(sig, down(sig, 0))
        if closed is None:
            face_up = up(face_down, None)
        else:
            face_up = jnp.where(row == closed[0], 0.0, harmonic(sig, up(sig, 0)))
            face_down = jnp.where(row == closed[1], 0.0, face_down)
        face_right = jnp.where(last, 0.0, harmonic(sig, right(sig)))
        face_left = left(face_right)
        diag = face_up + face_down + face_left + face_right + jnp.where(last, sig, 0.0) + (k * k) * sig
        inv = 1.0 / diag
        a_up, a_down, a_left, a_right = face_up * inv, face_down * inv, face_left * inv, face_right * inv

        def apply(v, tag):
            return a_up * up(v, tag) + a_down * down(v, tag) + a_left * left(v) + a_right * right(v)

        def begin(x, s):
            q = jnp.where((cell_row(row) + t * ROWS == srow_s[s]) & (col == scol_s[s]), SOURCE_STRENGTH, 0.0)
            return q * inv - x + apply(x, (s, 0))

        return diag, begin, apply

    def chains(work):
        v0 = [st[1](x, s) for st, x, s in work]
        v1 = [st[2](v, (s, 1)) for (st, _, s), v in zip(work, v0)]
        v2 = [st[2](v, (s, 2)) for (st, _, s), v in zip(work, v1)]
        v3 = [st[2](v, (s, 3)) for (st, _, s), v in zip(work, v2)]
        return list(zip(v0, v1, v2, v3))

    def fold(product):
        total = product[:, :LANES]
        for j in range(1, COLS // LANES):
            total = total + product[:, j * LANES:(j + 1) * LANES]
        return total

    def moments(d, v0, v1, v2, v3):
        d0, d1, d2 = d * v0, d * v1, d * v2
        return [fold(a * b) for a, b in ((d0, v0), (d0, v1), (d1, v1), (d1, v2), (d2, v2), (d2, v3))]

    sub = lax.broadcasted_iota(jnp.int32, (8, COLS), 0)
    upper = sub < 4
    upper_lanes = lax.broadcasted_iota(jnp.int32, (8, LANES), 0) < 4

    whole = stencil(
        sigma,
        lambda row: row,
        lambda v, tag: pltpu.roll(v, 1, 0),
        lambda v, tag: pltpu.roll(v, ROWS - 1, 0),
        None,
    )
    inner = chains([(whole, xbuf[s], s) for s in range(2)])
    inner_moments = [
        [f[8:16] + f[16:24] + jnp.where(upper_lanes, f[24:32], f[0:8]) for f in moments(whole[0], *inner[s])]
        for s in range(2)
    ]
    own = {0: (sigma[0:8], sigma[24:32])}
    for s in range(2):
        own[(s, 0)] = (xbuf[s, 0:8, :], xbuf[s, 24:32, :])
        for i in range(3):
            own[(s, i + 1)] = (inner[s][i][0:8], inner[s][i][24:32])

    electrode = ebuf[...].reshape(1, 64)
    electrode = jnp.concatenate([electrode, electrode], axis=1)
    here = lax.broadcasted_iota(jnp.int32, (ROWS, LANES), 0) + t * ROWS == electrode

    for copy in halos:
        copy.wait_recv()
    pl.semaphore_wait(known.at[1], len(middle))
    tell(known.at[2], far)

    edge_stencil = [
        stencil(
            jnp.where(upper, sigma[0:8], conductivity(halo_c[1])),
            lambda row: jnp.where(row < 4, row, row - 8),
            lambda v, tag: pltpu.roll(v, 1, 0),
            lambda v, tag: pltpu.roll(jnp.where(sub == 4, own[tag][0], v), 7, 0),
            (jnp.where(t == 0, 0, -1), jnp.where(t == 0, 7, -1)),
        ),
        stencil(
            jnp.where(upper, conductivity(halo_c[0]), sigma[24:32]),
            lambda row: jnp.where(row < 4, row + 32, row + 24),
            lambda v, tag: pltpu.roll(jnp.where(sub == 3, own[tag][1], v), 1, 0),
            lambda v, tag: pltpu.roll(v, 7, 0),
            (jnp.where(t == TILES - 1, 0, -1), jnp.where(t == TILES - 1, 7, -1)),
        ),
    ]
    outer = chains(
        [(edge_stencil[0], jnp.where(upper, own[(s, 0)][0], halo_x[1, s]), s) for s in range(2)]
        + [(edge_stencil[1], jnp.where(upper, halo_x[0, s], own[(s, 0)][1]), s) for s in range(2)]
    )
    edges = [(outer[s], outer[2 + s]) for s in range(2)]
    rows = []
    for s in range(2):
        pairs = zip(moments(edge_stencil[0][0], *edges[s][0]), moments(edge_stencil[1][0], *edges[s][1]))
        rows += [
            jnp.sum(a + jnp.where(upper_lanes, b, c), axis=0, keepdims=True)
            for a, (b, c) in zip(inner_moments[s], pairs)
        ]

    vectors = [
        [xbuf[s]]
        + [
            jnp.concatenate(
                [
                    jnp.where(upper, edges[s][0][i], inner[s][i][0:8]),
                    inner[s][i][8:24],
                    jnp.where(upper, inner[s][i][24:32], edges[s][1][i]),
                ],
                axis=0,
            )
            for i in range(3)
        ]
        for s in range(2)
    ]
    lane = lax.broadcasted_iota(jnp.int32, (1, LANES), 1)
    low = lane < 64
    surface = []
    for i in range(4):
        both = jnp.where(low, vectors[0][i][:, 0:1], vectors[1][i][:, 0:1])
        surface.append(jnp.sum(jnp.where(here, both, 0.0), axis=0, keepdims=True))
    surfaces[...] = jnp.concatenate(surface, axis=0)

    dots = jnp.sum(jnp.concatenate(rows, axis=0), axis=1, keepdims=True)
    eye = lax.broadcasted_iota(jnp.int32, (12, LANES), 0) == lax.broadcasted_iota(jnp.int32, (12, LANES), 1)
    packet[...] = jnp.sum(jnp.where(eye, dots, 0.0), axis=0, keepdims=True)
    peers = [tile_peer(step) for step in STEPS]
    for i, peer in enumerate(peers):
        remote(packet, slots.at[i], tile_send.at[0], tile_recv.at[0], peer).start()
    for i, peer in enumerate(peers):
        remote(surfaces, slots_e.at[i], tile_send.at[1], tile_recv.at[1], peer).start()

    every = remote(slots, slots, tile_send.at[0], tile_recv.at[0], (w, below))
    every_e = remote(slots_e, slots_e, tile_send.at[1], tile_recv.at[1], (w, below))
    every.wait_recv()
    total = packet[...] + jnp.sum(slots[...], axis=0)
    pl.semaphore_wait(known.at[2], len(far))

    weight = wt_s[0]
    coefs = []
    for s in range(2):
        nu = [jnp.broadcast_to(total[0:1, 6 * s + m:6 * s + m + 1], (1, LANES)) for m in range(6)]
        mu = [nu[m] - nu[m + 1] for m in range(5)]
        gamma0 = nu[0]
        alpha0 = gamma0 / mu[0]
        za, zb = 1.0 - alpha0, alpha0
        gamma1 = za * za * nu[0] + 2.0 * za * zb * nu[1] + zb * zb * nu[2]
        beta0 = gamma1 / gamma0
        pa, pb = za + beta0, zb
        curve1 = pa * pa * mu[0] + 2.0 * pa * pb * mu[1] + pb * pb * mu[2]
        alpha1 = gamma1 / curve1
        ya, yb, yc = za - alpha1 * pa, zb - alpha1 * (pb - pa), alpha1 * pb
        gamma2 = (
            ya * ya * nu[0] + yb * yb * nu[2] + yc * yc * nu[4]
            + 2.0 * (ya * yb * nu[1] + ya * yc * nu[2] + yb * yc * nu[3])
        )
        beta1 = gamma2 / gamma1
        ra, rb, rc = ya + beta1 * pa, yb + beta1 * pb, yc
        curve2 = (
            ra * ra * mu[0] + rb * rb * mu[2] + rc * rc * mu[4]
            + 2.0 * (ra * rb * mu[1] + ra * rc * mu[2] + rb * rc * mu[3])
        )
        alpha2 = gamma2 / curve2
        coefs.append((
            jnp.full((1, LANES), weight, jnp.float32),
            weight * (alpha0 + alpha1 * pa + alpha2 * ra),
            weight * (alpha1 * pb + alpha2 * rb),
            weight * (alpha2 * rc),
        ))

    low_rows = lax.broadcasted_iota(jnp.int32, (ROWS, LANES), 1) < 64
    for j in range(COLS // LANES):
        part = []
        for s in range(2):
            acc = vectors[s][0][:, j * LANES:(j + 1) * LANES] * coefs[s][0]
            for i in range(1, 4):
                acc = acc + vectors[s][i][:, j * LANES:(j + 1) * LANES] * coefs[s][i]
            part.append(acc)
        chunks[2 * j] = jnp.where(low_rows, part[0], pltpu.roll(part[1], 64, 1))
        chunks[2 * j + 1] = jnp.where(low_rows, pltpu.roll(part[0], 64, 1), part[1])

    copies_first = [
        remote(
            chunks.at[wave_peer(-o)[0]], got_first.at[i], first_send.at[i], first_recv.at[i], wave_peer(c - o)
        )
        for i, (c, o) in enumerate(FIRST_LIST)
    ]
    every_e.wait_recv()
    total_e = surfaces[...] + jnp.sum(slots_e[...], axis=0)
    mine[...] = sum(total_e[i:i + 1] * jnp.where(low, coefs[0][i], coefs[1][i]) for i in range(4))
    copies_r = [remote(mine, slots_r.at[i], r_send, r_recv, wave_peer(i + 1)) for i in range(WAVES - 1)]
    order = sorted(range(WAVES - 1), key=lambda i: -min(i + 1, WAVES - 1 - i))
    for i in order[:N_FAR_R]:
        copies_r[i].start()
    for copy in copies_first:
        copy.start()

    for i in order[N_FAR_R:]:
        copies_r[i].start()

    copies_second = []
    for j, c in enumerate(SECOND_LIST):
        acc = chunks[wave_peer(-c)[0]]
        for i, (cc, o) in enumerate(FIRST_LIST):
            if cc == c:
                copies_first[i].wait_recv()
                acc = acc + got_first[i]
        sums[j] = acc
        copy = remote(sums.at[j], got_second.at[j], second_send.at[j], second_recv.at[j], wave_peer(-c))
        copy.start()
        copies_second.append(copy)
    every_r = remote(slots_r, slots_r, r_send, r_recv, wave_peer(1))

    acc = chunks[w]
    for i, (c, o) in enumerate(FIRST_LIST):
        if c == 0:
            copies_first[i].wait_recv()
            acc = acc + got_first[i]
    for j in reversed(range(len(SECOND_LIST))):
        copies_second[j].wait_recv()
        acc = acc + got_second[j]
    pot[...] = acc

    every_r.wait_recv()
    read[...] = mine[...] + jnp.sum(slots_r[...], axis=0)

    for copy in halos + [every, every_e, every_r] + copies_first + copies_second:
        copy.wait_send()


def part(both, both_r, pot, read):
    pot[0] = both[:, :64]
    pot[1] = both[:, 64:]
    read[0:1, :] = both_r[:, :64]
    read[1:2, :] = both_r[:, 64:]


def shards(warm, cls, cond, wn, wt, srow, scol, erow):
    f32 = jnp.float32
    in_vmem = pl.BlockSpec(memory_space=pltpu.VMEM)
    dma = pltpu.SemaphoreType.DMA
    n_first, n_second = len(FIRST_LIST), len(SECOND_LIST)
    both = pl.pallas_call(
        kernel,
        out_shape=(
            jax.ShapeDtypeStruct((ROWS, LANES), f32),
            jax.ShapeDtypeStruct((1, LANES), f32),
        ),
        in_specs=[pl.BlockSpec(memory_space=pltpu.HBM)] * 8,
        out_specs=[in_vmem] * 2,
        scratch_shapes=[
            pltpu.VMEM((2, ROWS, COLS), f32),
            pltpu.VMEM((ROWS, COLS), jnp.int32),
            pltpu.VMEM((64,), jnp.int32),
            pltpu.SMEM((8,), f32),
            pltpu.SMEM((1,), f32),
            pltpu.SMEM((1,), f32),
            pltpu.SMEM((2,), jnp.int32),
            pltpu.SMEM((2,), jnp.int32),
            pltpu.VMEM((2, 8, COLS), jnp.int32),
            pltpu.VMEM((2, 2, 8, COLS), f32),
            pltpu.VMEM((1, LANES), f32),
            pltpu.VMEM((TILES - 1, 1, LANES), f32),
            pltpu.VMEM((4, LANES), f32),
            pltpu.VMEM((TILES - 1, 4, LANES), f32),
            pltpu.VMEM((WAVES, ROWS, LANES), f32),
            pltpu.VMEM((n_first, ROWS, LANES), f32),
            pltpu.VMEM((n_second, ROWS, LANES), f32),
            pltpu.VMEM((n_second, ROWS, LANES), f32),
            pltpu.VMEM((1, LANES), f32),
            pltpu.VMEM((WAVES - 1, 1, LANES), f32),
            dma((8,)),
            dma((4,)), dma((4,)),
            dma((2,)), dma((2,)),
            dma((n_first,)), dma((n_first,)),
            dma((n_second,)), dma((n_second,)),
            dma, dma,
            pltpu.SemaphoreType.REGULAR((3,)),
        ],
        compiler_params=pltpu.CompilerParams(
            collective_id=0, has_side_effects=True, vmem_limit_bytes=55168 * 1024
        ),
    )(warm, cls, cond, wn, wt, srow, scol, erow)
    return pl.pallas_call(
        part,
        out_shape=(
            jax.ShapeDtypeStruct((2, ROWS, COLS // WAVES), f32),
            jax.ShapeDtypeStruct((2, 64), f32),
        ),
        in_specs=[in_vmem] * 2,
        out_specs=[in_vmem] * 2,
        compiler_params=pltpu.CompilerParams(vmem_limit_bytes=55168 * 1024),
    )(*both)


def solution(mesh):
    return jax.shard_map(
        shards,
        mesh=mesh,
        in_specs=(
            P("wave", None, "tile", None), P("tile", None), P(), P("wave"), P("wave"), P(), P(), P(),
        ),
        out_specs=(P(None, "tile", "wave"), P()),
        check_vma=False,
    )
```

```python
import jax
import jax.numpy as jnp
from jax import lax
from jax.experimental import pallas as pl
from jax.experimental.pallas import tpu as pltpu
from jax.sharding import PartitionSpec as P

SOURCE_STRENGTH = 50.0
N_FAR_R = 7
MESH = pl.DeviceIdType.MESH

WAVES = 16
TILES = 32
ROWS = 32
COLS = 1024
LANES = 128

FIRST = {6: (8, 7, 5), -6: (-7, -5), 3: (4, 2), -3: (-4, -2), 0: (1, -1)}
FIRST_LIST = [(c, o) for c, offsets in FIRST.items() for o in offsets]
SECOND_LIST = [c for c in FIRST if c != 0]

STEPS = sorted(
    [(a, b, c) for a in range(4) for b in range(4) for c in range(2) if (a, b, c) != (0, 0, 0)],
    key=lambda s: -(min(s[0], 4 - s[0]) + min(s[1], 4 - s[1])),
)
NEAR = [s for s in STEPS if min(s[0], 4 - s[0]) + min(s[1], 4 - s[1]) <= 1]
FAR = [s for s in STEPS if min(s[0], 4 - s[0]) + min(s[1], 4 - s[1]) == 2 and s[2] == 0]


def harmonic(a, b):
    return 2.0 * a * b / (a + b)


def right(v):
    return pltpu.roll(v, COLS - 1, 1)


def left(v):
    return pltpu.roll(v, 1, 1)


def kernel(
    warm, cls, cond, wn, wt, srow, scol, erow,
    pot, read,
    xbuf, cbuf, ebuf, cond_s, wn_s, wt_s, srow_s, scol_s,
    halo_c, halo_x, packet, slots, surfaces, slots_e,
    chunks, got_first, sums, got_second, mine, slots_r,
    in_sem, halo_send, halo_recv, tile_send, tile_recv,
    first_send, first_recv, second_send, second_recv, r_send, r_recv,
    known,
):
    w = lax.axis_index("wave")
    t = lax.axis_index("tile")

    loads = [
        pltpu.make_async_copy(cls, cbuf, in_sem.at[0]),
        pltpu.make_async_copy(cond, cond_s, in_sem.at[1]),
        pltpu.make_async_copy(warm.at[0], xbuf, in_sem.at[2]),
        pltpu.make_async_copy(wn, wn_s, in_sem.at[3]),
        pltpu.make_async_copy(wt, wt_s, in_sem.at[4]),
        pltpu.make_async_copy(srow, srow_s, in_sem.at[5]),
        pltpu.make_async_copy(scol, scol_s, in_sem.at[6]),
        pltpu.make_async_copy(erow, ebuf, in_sem.at[7]),
    ]
    for load in loads:
        load.start()

    below = lax.rem(t + 1, TILES)
    above = lax.rem(t + TILES - 1, TILES)
    t_y, t_x, t_core = t // 8, lax.rem(t // 2, 4), lax.rem(t, 2)

    def tile_peer(step):
        dy, dx, dc = step
        return (w, lax.rem(t_y + dy, 4) * 8 + lax.rem(t_x + dx, 4) * 2 + lax.rem(t_core + dc, 2))

    def wave_peer(k):
        return (lax.rem(w + 2 * WAVES + k, WAVES), t)

    def tell(semaphore, peers):
        for peer in peers:
            pl.semaphore_signal(semaphore, inc=1, device_id=peer, device_id_type=MESH)

    near = [(w, below), (w, above)] + [tile_peer(s) for s in NEAR] + [wave_peer(1), wave_peer(-1)]
    middle = [tile_peer(s) for s in FAR] + [wave_peer(2), wave_peer(-2)]
    far = [wave_peer(4), wave_peer(-4)]
    barrier = pltpu.get_barrier_semaphore()
    tell(barrier, near)

    def remote(src, dst, send, recv, device):
        return pltpu.make_async_remote_copy(
            src_ref=src, dst_ref=dst, send_sem=send, recv_sem=recv, device_id=device, device_id_type=MESH
        )

    first, final = pl.ds(0, 8), pl.ds(ROWS - 8, 8)
    halos = [
        remote(cls.at[first], halo_c.at[0], halo_send.at[0], halo_recv.at[0], (w, above)),
        remote(cls.at[final], halo_c.at[1], halo_send.at[1], halo_recv.at[1], (w, below)),
        remote(warm.at[0, :, first], halo_x.at[0], halo_send.at[2], halo_recv.at[2], (w, above)),
        remote(warm.at[0, :, final], halo_x.at[1], halo_send.at[3], halo_recv.at[3], (w, below)),
    ]
    pl.semaphore_wait(barrier, len(near))
    for copy in halos:
        copy.start()
    tell(known.at[0], near)

    def conductivity(classes):
        value = jnp.full(classes.shape, cond_s[0], jnp.float32)
        for i in range(1, 8):
            value = jnp.where(classes == i, cond_s[i], value)
        return value

    for load in loads:
        load.wait()
    sigma = conductivity(cbuf[...])
    pl.semaphore_wait(known.at[0], len(near))
    tell(known.at[1], middle)

    k = wn_s[0]

    def stencil(sig, cell_row, up, down, closed):
        shape = sig.shape
        row = lax.broadcasted_iota(jnp.int32, shape, 0)
        col = lax.broadcasted_iota(jnp.int32, shape, 1)
        last = col == COLS - 1
        face_down = harmonic(sig, down(sig, 0))
        if closed is None:
            face_up = up(face_down, None)
        else:
            face_up = jnp.where(row == closed[0], 0.0, harmonic(sig, up(sig, 0)))
            face_down = jnp.where(row == closed[1], 0.0, face_down)
        face_right = jnp.where(last, 0.0, harmonic(sig, right(sig)))
        face_left = left(face_right)
        diag = face_up + face_down + face_left + face_right + jnp.where(last, sig, 0.0) + (k * k) * sig
        inv = 1.0 / diag
        a_up, a_down, a_left, a_right = face_up * inv, face_down * inv, face_left * inv, face_right * inv

        def apply(v, tag):
            return a_up * up(v, tag) + a_down * down(v, tag) + a_left * left(v) + a_right * right(v)

        def begin(x, s):
            q = jnp.where((cell_row(row) + t * ROWS == srow_s[s]) & (col == scol_s[s]), SOURCE_STRENGTH, 0.0)
            return q * inv - x + apply(x, (s, 0))

        return diag, begin, apply

    def chains(work):
        v0 = [st[1](x, s) for st, x, s in work]
        v1 = [st[2](v, (s, 1)) for (st, _, s), v in zip(work, v0)]
        v2 = [st[2](v, (s, 2)) for (st, _, s), v in zip(work, v1)]
        v3 = [st[2](v, (s, 3)) for (st, _, s), v in zip(work, v2)]
        return list(zip(v0, v1, v2, v3))

    def fold(product):
        total = product[:, :LANES]
        for j in range(1, COLS // LANES):
            total = total + product[:, j * LANES:(j + 1) * LANES]
        return total

    def moments(d, v0, v1, v2, v3):
        d0, d1, d2 = d * v0, d * v1, d * v2
        return [fold(a * b) for a, b in ((d0, v0), (d0, v1), (d1, v1), (d1, v2), (d2, v2), (d2, v3))]

    sub = lax.broadcasted_iota(jnp.int32, (8, COLS), 0)
    upper = sub < 4
    upper_lanes = lax.broadcasted_iota(jnp.int32, (8, LANES), 0) < 4

    whole = stencil(
        sigma,
        lambda row: row,
        lambda v, tag: pltpu.roll(v, 1, 0),
        lambda v, tag: pltpu.roll(v, ROWS - 1, 0),
        None,
    )
    inner = chains([(whole, xbuf[s], s) for s in range(2)])
    inner_moments = [
        [f[8:16] + f[16:24] + jnp.where(upper_lanes, f[24:32], f[0:8]) for f in moments(whole[0], *inner[s])]
        for s in range(2)
    ]
    own = {0: (sigma[0:8], sigma[24:32])}
    for s in range(2):
        own[(s, 0)] = (xbuf[s, 0:8, :], xbuf[s, 24:32, :])
        for i in range(3):
            own[(s, i + 1)] = (inner[s][i][0:8], inner[s][i][24:32])

    electrode = ebuf[...].reshape(1, 64)
    electrode = jnp.concatenate([electrode, electrode], axis=1)
    here = lax.broadcasted_iota(jnp.int32, (ROWS, LANES), 0) + t * ROWS == electrode

    for copy in halos:
        copy.wait_recv()
    pl.semaphore_wait(known.at[1], len(middle))
    tell(known.at[2], far)

    edge_stencil = [
        stencil(
            jnp.where(upper, sigma[0:8], conductivity(halo_c[1])),
            lambda row: jnp.where(row < 4, row, row - 8),
            lambda v, tag: pltpu.roll(v, 1, 0),
            lambda v, tag: pltpu.roll(jnp.where(sub == 4, own[tag][0], v), 7, 0),
            (jnp.where(t == 0, 0, -1), jnp.where(t == 0, 7, -1)),
        ),
        stencil(
            jnp.where(upper, conductivity(halo_c[0]), sigma[24:32]),
            lambda row: jnp.where(row < 4, row + 32, row + 24),
            lambda v, tag: pltpu.roll(jnp.where(sub == 3, own[tag][1], v), 1, 0),
            lambda v, tag: pltpu.roll(v, 7, 0),
            (jnp.where(t == TILES - 1, 0, -1), jnp.where(t == TILES - 1, 7, -1)),
        ),
    ]
    outer = chains(
        [(edge_stencil[0], jnp.where(upper, own[(s, 0)][0], halo_x[1, s]), s) for s in range(2)]
        + [(edge_stencil[1], jnp.where(upper, halo_x[0, s], own[(s, 0)][1]), s) for s in range(2)]
    )
    edges = [(outer[s], outer[2 + s]) for s in range(2)]
    rows = []
    for s in range(2):
        pairs = zip(moments(edge_stencil[0][0], *edges[s][0]), moments(edge_stencil[1][0], *edges[s][1]))
        rows += [
            jnp.sum(a + jnp.where(upper_lanes, b, c), axis=0, keepdims=True)
            for a, (b, c) in zip(inner_moments[s], pairs)
        ]

    vectors = [
        [xbuf[s]]
        + [
            jnp.concatenate(
                [
                    jnp.where(upper, edges[s][0][i], inner[s][i][0:8]),
                    inner[s][i][8:24],
                    jnp.where(upper, inner[s][i][24:32], edges[s][1][i]),
                ],
                axis=0,
            )
            for i in range(3)
        ]
        for s in range(2)
    ]
    lane = lax.broadcasted_iota(jnp.int32, (1, LANES), 1)
    low = lane < 64
    surface = []
    for i in range(4):
        both = jnp.where(low, vectors[0][i][:, 0:1], vectors[1][i][:, 0:1])
        surface.append(jnp.sum(jnp.where(here, both, 0.0), axis=0, keepdims=True))
    surfaces[...] = jnp.concatenate(surface, axis=0)

    dots = jnp.sum(jnp.concatenate(rows, axis=0), axis=1, keepdims=True)
    eye = lax.broadcasted_iota(jnp.int32, (12, LANES), 0) == lax.broadcasted_iota(jnp.int32, (12, LANES), 1)
    packet[...] = jnp.sum(jnp.where(eye, dots, 0.0), axis=0, keepdims=True)
    peers = [tile_peer(step) for step in STEPS]
    for i, peer in enumerate(peers):
        remote(packet, slots.at[i], tile_send.at[0], tile_recv.at[0], peer).start()
    for i, peer in enumerate(peers):
        remote(surfaces, slots_e.at[i], tile_send.at[1], tile_recv.at[1], peer).start()

    every = remote(slots, slots, tile_send.at[0], tile_recv.at[0], (w, below))
    every_e = remote(slots_e, slots_e, tile_send.at[1], tile_recv.at[1], (w, below))
    every.wait_recv()
    total = packet[...] + jnp.sum(slots[...], axis=0)
    pl.semaphore_wait(known.at[2], len(far))

    weight = wt_s[0]
    coefs = []
    for s in range(2):
        nu = [jnp.broadcast_to(total[0:1, 6 * s + m:6 * s + m + 1], (1, LANES)) for m in range(6)]
        mu = [nu[m] - nu[m + 1] for m in range(5)]
        gamma0 = nu[0]
        alpha0 = gamma0 / mu[0]
        za, zb = 1.0 - alpha0, alpha0
        gamma1 = za * za * nu[0] + 2.0 * za * zb * nu[1] + zb * zb * nu[2]
        beta0 = gamma1 / gamma0
        pa, pb = za + beta0, zb
        curve1 = pa * pa * mu[0] + 2.0 * pa * pb * mu[1] + pb * pb * mu[2]
        alpha1 = gamma1 / curve1
        ya, yb, yc = za - alpha1 * pa, zb - alpha1 * (pb - pa), alpha1 * pb
        gamma2 = (
            ya * ya * nu[0] + yb * yb * nu[2] + yc * yc * nu[4]
            + 2.0 * (ya * yb * nu[1] + ya * yc * nu[2] + yb * yc * nu[3])
        )
        beta1 = gamma2 / gamma1
        ra, rb, rc = ya + beta1 * pa, yb + beta1 * pb, yc
        curve2 = (
            ra * ra * mu[0] + rb * rb * mu[2] + rc * rc * mu[4]
            + 2.0 * (ra * rb * mu[1] + ra * rc * mu[2] + rb * rc * mu[3])
        )
        alpha2 = gamma2 / curve2
        coefs.append((
            jnp.full((1, LANES), weight, jnp.float32),
            weight * (alpha0 + alpha1 * pa + alpha2 * ra),
            weight * (alpha1 * pb + alpha2 * rb),
            weight * (alpha2 * rc),
        ))

    low_rows = lax.broadcasted_iota(jnp.int32, (ROWS, LANES), 1) < 64
    for j in range(COLS // LANES):
        part = []
        for s in range(2):
            acc = vectors[s][0][:, j * LANES:(j + 1) * LANES] * coefs[s][0]
            for i in range(1, 4):
                acc = acc + vectors[s][i][:, j * LANES:(j + 1) * LANES] * coefs[s][i]
            part.append(acc)
        chunks[2 * j] = jnp.where(low_rows, part[0], pltpu.roll(part[1], 64, 1))
        chunks[2 * j + 1] = jnp.where(low_rows, pltpu.roll(part[0], 64, 1), part[1])

    copies_first = [
        remote(
            chunks.at[wave_peer(-o)[0]], got_first.at[i], first_send.at[i], first_recv.at[i], wave_peer(c - o)
        )
        for i, (c, o) in enumerate(FIRST_LIST)
    ]
    for copy in copies_first:
        copy.start()
    every_e.wait_recv()
    total_e = surfaces[...] + jnp.sum(slots_e[...], axis=0)
    mine[...] = sum(total_e[i:i + 1] * jnp.where(low, coefs[0][i], coefs[1][i]) for i in range(4))
    copies_r = [remote(mine, slots_r.at[i], r_send, r_recv, wave_peer(i + 1)) for i in range(WAVES - 1)]
    order = sorted(range(WAVES - 1), key=lambda i: -min(i + 1, WAVES - 1 - i))
    for i in order[:N_FAR_R]:
        copies_r[i].start()

    for i in order[N_FAR_R:]:
        copies_r[i].start()

    copies_second = []
    for j, c in enumerate(SECOND_LIST):
        acc = chunks[wave_peer(-c)[0]]
        for i, (cc, o) in enumerate(FIRST_LIST):
            if cc == c:
                copies_first[i].wait_recv()
                acc = acc + got_first[i]
        sums[j] = acc
        copy = remote(sums.at[j], got_second.at[j], second_send.at[j], second_recv.at[j], wave_peer(-c))
        copy.start()
        copies_second.append(copy)
    every_r = remote(slots_r, slots_r, r_send, r_recv, wave_peer(1))

    acc = chunks[w]
    for i, (c, o) in enumerate(FIRST_LIST):
        if c == 0:
            copies_first[i].wait_recv()
            acc = acc + got_first[i]
    for j in reversed(range(len(SECOND_LIST))):
        copies_second[j].wait_recv()
        acc = acc + got_second[j]
    pot[...] = acc

    every_r.wait_recv()
    read[...] = mine[...] + jnp.sum(slots_r[...], axis=0)

    for copy in halos + [every, every_e, every_r] + copies_first + copies_second:
        copy.wait_send()


def part(both, both_r, pot, read):
    pot[0] = both[:, :64]
    pot[1] = both[:, 64:]
    read[0:1, :] = both_r[:, :64]
    read[1:2, :] = both_r[:, 64:]


def shards(warm, cls, cond, wn, wt, srow, scol, erow):
    f32 = jnp.float32
    in_vmem = pl.BlockSpec(memory_space=pltpu.VMEM)
    dma = pltpu.SemaphoreType.DMA
    n_first, n_second = len(FIRST_LIST), len(SECOND_LIST)
    both = pl.pallas_call(
        kernel,
        out_shape=(
            jax.ShapeDtypeStruct((ROWS, LANES), f32),
            jax.ShapeDtypeStruct((1, LANES), f32),
        ),
        in_specs=[pl.BlockSpec(memory_space=pltpu.HBM)] * 8,
        out_specs=[in_vmem] * 2,
        scratch_shapes=[
            pltpu.VMEM((2, ROWS, COLS), f32),
            pltpu.VMEM((ROWS, COLS), jnp.int32),
            pltpu.VMEM((64,), jnp.int32),
            pltpu.SMEM((8,), f32),
            pltpu.SMEM((1,), f32),
            pltpu.SMEM((1,), f32),
            pltpu.SMEM((2,), jnp.int32),
            pltpu.SMEM((2,), jnp.int32),
            pltpu.VMEM((2, 8, COLS), jnp.int32),
            pltpu.VMEM((2, 2, 8, COLS), f32),
            pltpu.VMEM((1, LANES), f32),
            pltpu.VMEM((TILES - 1, 1, LANES), f32),
            pltpu.VMEM((4, LANES), f32),
            pltpu.VMEM((TILES - 1, 4, LANES), f32),
            pltpu.VMEM((WAVES, ROWS, LANES), f32),
            pltpu.VMEM((n_first, ROWS, LANES), f32),
            pltpu.VMEM((n_second, ROWS, LANES), f32),
            pltpu.VMEM((n_second, ROWS, LANES), f32),
            pltpu.VMEM((1, LANES), f32),
            pltpu.VMEM((WAVES - 1, 1, LANES), f32),
            dma((8,)),
            dma((4,)), dma((4,)),
            dma((2,)), dma((2,)),
            dma((n_first,)), dma((n_first,)),
            dma((n_second,)), dma((n_second,)),
            dma, dma,
            pltpu.SemaphoreType.REGULAR((3,)),
        ],
        compiler_params=pltpu.CompilerParams(
            collective_id=0, has_side_effects=True, vmem_limit_bytes=55168 * 1024
        ),
    )(warm, cls, cond, wn, wt, srow, scol, erow)
    return pl.pallas_call(
        part,
        out_shape=(
            jax.ShapeDtypeStruct((2, ROWS, COLS // WAVES), f32),
            jax.ShapeDtypeStruct((2, 64), f32),
        ),
        in_specs=[in_vmem] * 2,
        out_specs=[in_vmem] * 2,
        compiler_params=pltpu.CompilerParams(vmem_limit_bytes=55168 * 1024),
    )(*both)


def solution(mesh):
    return jax.shard_map(
        shards,
        mesh=mesh,
        in_specs=(
            P("wave", None, "tile", None), P("tile", None), P(), P("wave"), P("wave"), P(), P(), P(),
        ),
        out_specs=(P(None, "tile", "wave"), P()),
        check_vma=False,
    )
```

```python
import jax
import jax.numpy as jnp
from jax import lax
from jax.experimental import pallas as pl
from jax.experimental.pallas import tpu as pltpu
from jax.sharding import PartitionSpec as P

SOURCE_STRENGTH = 50.0
N_FAR_R = 7
MESH = pl.DeviceIdType.MESH

WAVES = 16
TILES = 32
ROWS = 32
COLS = 1024
LANES = 128

FIRST = {6: (8, 7, 5), -6: (-7, -5), 3: (4, 2), -3: (-4, -2), 0: (1, -1)}
FIRST_LIST = [(c, o) for c, offsets in FIRST.items() for o in offsets]
SECOND_LIST = [c for c in FIRST if c != 0]

STEPS = sorted(
    [(a, b, c) for a in range(4) for b in range(4) for c in range(2) if (a, b, c) != (0, 0, 0)],
    key=lambda s: -(min(s[0], 4 - s[0]) + min(s[1], 4 - s[1])),
)
NEAR = [s for s in STEPS if min(s[0], 4 - s[0]) + min(s[1], 4 - s[1]) <= 1]
FAR = [s for s in STEPS if min(s[0], 4 - s[0]) + min(s[1], 4 - s[1]) == 2 and s[2] == 0]


def harmonic(a, b):
    return 2.0 * a * b / (a + b)


def right(v):
    return pltpu.roll(v, COLS - 1, 1)


def left(v):
    return pltpu.roll(v, 1, 1)


def kernel(
    warm, cls, cond, wn, wt, srow, scol, erow,
    pot, read,
    xbuf, cbuf, ebuf, cond_s, wn_s, wt_s, srow_s, scol_s,
    halo_c, halo_x, packet, slots, surfaces, slots_e,
    chunks, got_first, sums, got_second, mine, slots_r,
    in_sem, halo_send, halo_recv, tile_send, tile_recv,
    first_send, first_recv, second_send, second_recv, r_send, r_recv,
    known,
):
    w = lax.axis_index("wave")
    t = lax.axis_index("tile")

    loads = [
        pltpu.make_async_copy(cls, cbuf, in_sem.at[0]),
        pltpu.make_async_copy(cond, cond_s, in_sem.at[1]),
        pltpu.make_async_copy(warm.at[0], xbuf, in_sem.at[2]),
        pltpu.make_async_copy(wn, wn_s, in_sem.at[3]),
        pltpu.make_async_copy(wt, wt_s, in_sem.at[4]),
        pltpu.make_async_copy(srow, srow_s, in_sem.at[5]),
        pltpu.make_async_copy(scol, scol_s, in_sem.at[6]),
        pltpu.make_async_copy(erow, ebuf, in_sem.at[7]),
    ]
    for load in loads:
        load.start()

    below = lax.rem(t + 1, TILES)
    above = lax.rem(t + TILES - 1, TILES)
    t_y, t_x, t_core = t // 8, lax.rem(t // 2, 4), lax.rem(t, 2)

    def tile_peer(step):
        dy, dx, dc = step
        return (w, lax.rem(t_y + dy, 4) * 8 + lax.rem(t_x + dx, 4) * 2 + lax.rem(t_core + dc, 2))

    def wave_peer(k):
        return (lax.rem(w + 2 * WAVES + k, WAVES), t)

    def tell(semaphore, peers):
        for peer in peers:
            pl.semaphore_signal(semaphore, inc=1, device_id=peer, device_id_type=MESH)

    near = [(w, below), (w, above)] + [tile_peer(s) for s in NEAR] + [wave_peer(1), wave_peer(-1)]
    middle = [tile_peer(s) for s in FAR] + [wave_peer(2), wave_peer(-2)]
    far = [wave_peer(4), wave_peer(-4)]
    barrier = pltpu.get_barrier_semaphore()
    tell(barrier, near)

    def remote(src, dst, send, recv, device):
        return pltpu.make_async_remote_copy(
            src_ref=src, dst_ref=dst, send_sem=send, recv_sem=recv, device_id=device, device_id_type=MESH
        )

    first, final = pl.ds(0, 8), pl.ds(ROWS - 8, 8)
    halos = [
        remote(cls.at[first], halo_c.at[0], halo_send.at[0], halo_recv.at[0], (w, above)),
        remote(cls.at[final], halo_c.at[1], halo_send.at[1], halo_recv.at[1], (w, below)),
        remote(warm.at[0, :, first], halo_x.at[0], halo_send.at[2], halo_recv.at[2], (w, above)),
        remote(warm.at[0, :, final], halo_x.at[1], halo_send.at[3], halo_recv.at[3], (w, below)),
    ]
    pl.semaphore_wait(barrier, len(near))
    for copy in halos:
        copy.start()
    tell(known.at[0], near)

    def conductivity(classes):
        value = jnp.full(classes.shape, cond_s[0], jnp.float32)
        for i in range(1, 8):
            value = jnp.where(classes == i, cond_s[i], value)
        return value

    for load in loads:
        load.wait()
    sigma = conductivity(cbuf[...])
    pl.semaphore_wait(known.at[0], len(near))
    tell(known.at[1], middle)

    k = wn_s[0]

    def stencil(sig, cell_row, up, down, closed):
        shape = sig.shape
        row = lax.broadcasted_iota(jnp.int32, shape, 0)
        col = lax.broadcasted_iota(jnp.int32, shape, 1)
        last = col == COLS - 1
        face_down = harmonic(sig, down(sig, 0))
        if closed is None:
            face_up = up(face_down, None)
        else:
            face_up = jnp.where(row == closed[0], 0.0, harmonic(sig, up(sig, 0)))
            face_down = jnp.where(row == closed[1], 0.0, face_down)
        face_right = jnp.where(last, 0.0, harmonic(sig, right(sig)))
        face_left = left(face_right)
        diag = face_up + face_down + face_left + face_right + jnp.where(last, sig, 0.0) + (k * k) * sig
        inv = 1.0 / diag
        a_up, a_down, a_left, a_right = face_up * inv, face_down * inv, face_left * inv, face_right * inv

        def apply(v, tag):
            return a_up * up(v, tag) + a_down * down(v, tag) + a_left * left(v) + a_right * right(v)

        def begin(x, s):
            q = jnp.where((cell_row(row) + t * ROWS == srow_s[s]) & (col == scol_s[s]), SOURCE_STRENGTH, 0.0)
            return q * inv - x + apply(x, (s, 0))

        return diag, begin, apply

    def chains(work):
        v0 = [st[1](x, s) for st, x, s in work]
        v1 = [st[2](v, (s, 1)) for (st, _, s), v in zip(work, v0)]
        v2 = [st[2](v, (s, 2)) for (st, _, s), v in zip(work, v1)]
        v3 = [st[2](v, (s, 3)) for (st, _, s), v in zip(work, v2)]
        return list(zip(v0, v1, v2, v3))

    def fold(product):
        total = product[:, :LANES]
        for j in range(1, COLS // LANES):
            total = total + product[:, j * LANES:(j + 1) * LANES]
        return total

    def moments(d, v0, v1, v2, v3):
        d0, d1, d2 = d * v0, d * v1, d * v2
        return [fold(a * b) for a, b in ((d0, v0), (d0, v1), (d1, v1), (d1, v2), (d2, v2), (d2, v3))]

    sub = lax.broadcasted_iota(jnp.int32, (8, COLS), 0)
    upper = sub < 4
    upper_lanes = lax.broadcasted_iota(jnp.int32, (8, LANES), 0) < 4

    whole = stencil(
        sigma,
        lambda row: row,
        lambda v, tag: pltpu.roll(v, 1, 0),
        lambda v, tag: pltpu.roll(v, ROWS - 1, 0),
        None,
    )
    inner = chains([(whole, xbuf[s], s) for s in range(2)])
    inner_moments = [
        [f[8:16] + f[16:24] + jnp.where(upper_lanes, f[24:32], f[0:8]) for f in moments(whole[0], *inner[s])]
        for s in range(2)
    ]
    own = {0: (sigma[0:8], sigma[24:32])}
    for s in range(2):
        own[(s, 0)] = (xbuf[s, 0:8, :], xbuf[s, 24:32, :])
        for i in range(3):
            own[(s, i + 1)] = (inner[s][i][0:8], inner[s][i][24:32])

    electrode = ebuf[...].reshape(1, 64)
    electrode = jnp.concatenate([electrode, electrode], axis=1)
    here = lax.broadcasted_iota(jnp.int32, (ROWS, LANES), 0) + t * ROWS == electrode

    for copy in halos:
        copy.wait_recv()
    pl.semaphore_wait(known.at[1], len(middle))
    tell(known.at[2], far)

    edge_stencil = [
        stencil(
            jnp.where(upper, sigma[0:8], conductivity(halo_c[1])),
            lambda row: jnp.where(row < 4, row, row - 8),
            lambda v, tag: pltpu.roll(v, 1, 0),
            lambda v, tag: pltpu.roll(jnp.where(sub == 4, own[tag][0], v), 7, 0),
            (jnp.where(t == 0, 0, -1), jnp.where(t == 0, 7, -1)),
        ),
        stencil(
            jnp.where(upper, conductivity(halo_c[0]), sigma[24:32]),
            lambda row: jnp.where(row < 4, row + 32, row + 24),
            lambda v, tag: pltpu.roll(jnp.where(sub == 3, own[tag][1], v), 1, 0),
            lambda v, tag: pltpu.roll(v, 7, 0),
            (jnp.where(t == TILES - 1, 0, -1), jnp.where(t == TILES - 1, 7, -1)),
        ),
    ]
    outer = chains(
        [(edge_stencil[0], jnp.where(upper, own[(s, 0)][0], halo_x[1, s]), s) for s in range(2)]
        + [(edge_stencil[1], jnp.where(upper, halo_x[0, s], own[(s, 0)][1]), s) for s in range(2)]
    )
    edges = [(outer[s], outer[2 + s]) for s in range(2)]
    rows = []
    for s in range(2):
        pairs = zip(moments(edge_stencil[0][0], *edges[s][0]), moments(edge_stencil[1][0], *edges[s][1]))
        rows += [
            jnp.sum(a + jnp.where(upper_lanes, b, c), axis=0, keepdims=True)
            for a, (b, c) in zip(inner_moments[s], pairs)
        ]

    dots = jnp.sum(jnp.concatenate(rows, axis=0), axis=1, keepdims=True)
    eye = lax.broadcasted_iota(jnp.int32, (12, LANES), 0) == lax.broadcasted_iota(jnp.int32, (12, LANES), 1)
    packet[...] = jnp.sum(jnp.where(eye, dots, 0.0), axis=0, keepdims=True)
    peers = [tile_peer(step) for step in STEPS]
    for i, peer in enumerate(peers):
        remote(packet, slots.at[i], tile_send.at[0], tile_recv.at[0], peer).start()
    vectors = [
        [xbuf[s]]
        + [
            jnp.concatenate(
                [
                    jnp.where(upper, edges[s][0][i], inner[s][i][0:8]),
                    inner[s][i][8:24],
                    jnp.where(upper, inner[s][i][24:32], edges[s][1][i]),
                ],
                axis=0,
            )
            for i in range(3)
        ]
        for s in range(2)
    ]
    lane = lax.broadcasted_iota(jnp.int32, (1, LANES), 1)
    low = lane < 64
    surface = []
    for i in range(4):
        both = jnp.where(low, vectors[0][i][:, 0:1], vectors[1][i][:, 0:1])
        surface.append(jnp.sum(jnp.where(here, both, 0.0), axis=0, keepdims=True))
    surfaces[...] = jnp.concatenate(surface, axis=0)
    for i, peer in enumerate(peers):
        remote(surfaces, slots_e.at[i], tile_send.at[1], tile_recv.at[1], peer).start()

    every = remote(slots, slots, tile_send.at[0], tile_recv.at[0], (w, below))
    every_e = remote(slots_e, slots_e, tile_send.at[1], tile_recv.at[1], (w, below))
    every.wait_recv()
    total = packet[...] + jnp.sum(slots[...], axis=0)
    pl.semaphore_wait(known.at[2], len(far))

    weight = wt_s[0]
    coefs = []
    for s in range(2):
        nu = [jnp.broadcast_to(total[0:1, 6 * s + m:6 * s + m + 1], (1, LANES)) for m in range(6)]
        mu = [nu[m] - nu[m + 1] for m in range(5)]
        gamma0 = nu[0]
        alpha0 = gamma0 / mu[0]
        za, zb = 1.0 - alpha0, alpha0
        gamma1 = za * za * nu[0] + 2.0 * za * zb * nu[1] + zb * zb * nu[2]
        beta0 = gamma1 / gamma0
        pa, pb = za + beta0, zb
        curve1 = pa * pa * mu[0] + 2.0 * pa * pb * mu[1] + pb * pb * mu[2]
        alpha1 = gamma1 / curve1
        ya, yb, yc = za - alpha1 * pa, zb - alpha1 * (pb - pa), alpha1 * pb
        gamma2 = (
            ya * ya * nu[0] + yb * yb * nu[2] + yc * yc * nu[4]
            + 2.0 * (ya * yb * nu[1] + ya * yc * nu[2] + yb * yc * nu[3])
        )
        beta1 = gamma2 / gamma1
        ra, rb, rc = ya + beta1 * pa, yb + beta1 * pb, yc
        curve2 = (
            ra * ra * mu[0] + rb * rb * mu[2] + rc * rc * mu[4]
            + 2.0 * (ra * rb * mu[1] + ra * rc * mu[2] + rb * rc * mu[3])
        )
        alpha2 = gamma2 / curve2
        coefs.append((
            jnp.full((1, LANES), weight, jnp.float32),
            weight * (alpha0 + alpha1 * pa + alpha2 * ra),
            weight * (alpha1 * pb + alpha2 * rb),
            weight * (alpha2 * rc),
        ))

    low_rows = lax.broadcasted_iota(jnp.int32, (ROWS, LANES), 1) < 64
    for j in range(COLS // LANES):
        part = []
        for s in range(2):
            acc = vectors[s][0][:, j * LANES:(j + 1) * LANES] * coefs[s][0]
            for i in range(1, 4):
                acc = acc + vectors[s][i][:, j * LANES:(j + 1) * LANES] * coefs[s][i]
            part.append(acc)
        chunks[2 * j] = jnp.where(low_rows, part[0], pltpu.roll(part[1], 64, 1))
        chunks[2 * j + 1] = jnp.where(low_rows, pltpu.roll(part[0], 64, 1), part[1])

    copies_first = [
        remote(
            chunks.at[wave_peer(-o)[0]], got_first.at[i], first_send.at[i], first_recv.at[i], wave_peer(c - o)
        )
        for i, (c, o) in enumerate(FIRST_LIST)
    ]
    for copy in copies_first:
        copy.start()
    every_e.wait_recv()
    total_e = surfaces[...] + jnp.sum(slots_e[...], axis=0)
    mine[...] = sum(total_e[i:i + 1] * jnp.where(low, coefs[0][i], coefs[1][i]) for i in range(4))
    copies_r = [remote(mine, slots_r.at[i], r_send, r_recv, wave_peer(i + 1)) for i in range(WAVES - 1)]
    order = sorted(range(WAVES - 1), key=lambda i: -min(i + 1, WAVES - 1 - i))
    for i in order[:N_FAR_R]:
        copies_r[i].start()

    for i in order[N_FAR_R:]:
        copies_r[i].start()

    copies_second = []
    for j, c in enumerate(SECOND_LIST):
        acc = chunks[wave_peer(-c)[0]]
        for i, (cc, o) in enumerate(FIRST_LIST):
            if cc == c:
                copies_first[i].wait_recv()
                acc = acc + got_first[i]
        sums[j] = acc
        copy = remote(sums.at[j], got_second.at[j], second_send.at[j], second_recv.at[j], wave_peer(-c))
        copy.start()
        copies_second.append(copy)
    every_r = remote(slots_r, slots_r, r_send, r_recv, wave_peer(1))

    acc = chunks[w]
    for i, (c, o) in enumerate(FIRST_LIST):
        if c == 0:
            copies_first[i].wait_recv()
            acc = acc + got_first[i]
    for j in reversed(range(len(SECOND_LIST))):
        copies_second[j].wait_recv()
        acc = acc + got_second[j]
    pot[...] = acc

    every_r.wait_recv()
    read[...] = mine[...] + jnp.sum(slots_r[...], axis=0)

    for copy in halos + [every, every_e, every_r] + copies_first + copies_second:
        copy.wait_send()


def part(both, both_r, pot, read):
    pot[0] = both[:, :64]
    pot[1] = both[:, 64:]
    read[0:1, :] = both_r[:, :64]
    read[1:2, :] = both_r[:, 64:]


def shards(warm, cls, cond, wn, wt, srow, scol, erow):
    f32 = jnp.float32
    in_vmem = pl.BlockSpec(memory_space=pltpu.VMEM)
    dma = pltpu.SemaphoreType.DMA
    n_first, n_second = len(FIRST_LIST), len(SECOND_LIST)
    both = pl.pallas_call(
        kernel,
        out_shape=(
            jax.ShapeDtypeStruct((ROWS, LANES), f32),
            jax.ShapeDtypeStruct((1, LANES), f32),
        ),
        in_specs=[pl.BlockSpec(memory_space=pltpu.HBM)] * 8,
        out_specs=[in_vmem] * 2,
        scratch_shapes=[
            pltpu.VMEM((2, ROWS, COLS), f32),
            pltpu.VMEM((ROWS, COLS), jnp.int32),
            pltpu.VMEM((64,), jnp.int32),
            pltpu.SMEM((8,), f32),
            pltpu.SMEM((1,), f32),
            pltpu.SMEM((1,), f32),
            pltpu.SMEM((2,), jnp.int32),
            pltpu.SMEM((2,), jnp.int32),
            pltpu.VMEM((2, 8, COLS), jnp.int32),
            pltpu.VMEM((2, 2, 8, COLS), f32),
            pltpu.VMEM((1, LANES), f32),
            pltpu.VMEM((TILES - 1, 1, LANES), f32),
            pltpu.VMEM((4, LANES), f32),
            pltpu.VMEM((TILES - 1, 4, LANES), f32),
            pltpu.VMEM((WAVES, ROWS, LANES), f32),
            pltpu.VMEM((n_first, ROWS, LANES), f32),
            pltpu.VMEM((n_second, ROWS, LANES), f32),
            pltpu.VMEM((n_second, ROWS, LANES), f32),
            pltpu.VMEM((1, LANES), f32),
            pltpu.VMEM((WAVES - 1, 1, LANES), f32),
            dma((8,)),
            dma((4,)), dma((4,)),
            dma((2,)), dma((2,)),
            dma((n_first,)), dma((n_first,)),
            dma((n_second,)), dma((n_second,)),
            dma, dma,
            pltpu.SemaphoreType.REGULAR((3,)),
        ],
        compiler_params=pltpu.CompilerParams(
            collective_id=0, has_side_effects=True, vmem_limit_bytes=55168 * 1024
        ),
    )(warm, cls, cond, wn, wt, srow, scol, erow)
    return pl.pallas_call(
        part,
        out_shape=(
            jax.ShapeDtypeStruct((2, ROWS, COLS // WAVES), f32),
            jax.ShapeDtypeStruct((2, 64), f32),
        ),
        in_specs=[in_vmem] * 2,
        out_specs=[in_vmem] * 2,
        compiler_params=pltpu.CompilerParams(vmem_limit_bytes=55168 * 1024),
    )(*both)


def solution(mesh):
    return jax.shard_map(
        shards,
        mesh=mesh,
        in_specs=(
            P("wave", None, "tile", None), P("tile", None), P(), P("wave"), P("wave"), P(), P(), P(),
        ),
        out_specs=(P(None, "tile", "wave"), P()),
        check_vma=False,
    )
```

```python
import jax
import jax.numpy as jnp
from jax import lax
from jax.experimental import pallas as pl
from jax.experimental.pallas import tpu as pltpu
from jax.sharding import PartitionSpec as P

SOURCE_STRENGTH = 50.0
N_FAR_R = 7
MESH = pl.DeviceIdType.MESH

WAVES = 16
TILES = 32
ROWS = 32
COLS = 1024
LANES = 128

FIRST = {6: (8, 7, 5), -6: (-7, -5), 3: (4, 2), -3: (-4, -2), 0: (1, -1)}
FIRST_LIST = [(c, o) for c, offsets in FIRST.items() for o in offsets]
SECOND_LIST = [c for c in FIRST if c != 0]

STEPS = sorted(
    [(a, b, c) for a in range(4) for b in range(4) for c in range(2) if (a, b, c) != (0, 0, 0)],
    key=lambda s: -(min(s[0], 4 - s[0]) + min(s[1], 4 - s[1])),
)
NEAR = [s for s in STEPS if min(s[0], 4 - s[0]) + min(s[1], 4 - s[1]) <= 1]
FAR = [s for s in STEPS if min(s[0], 4 - s[0]) + min(s[1], 4 - s[1]) == 2 and s[2] == 0]


def harmonic(a, b):
    return 2.0 * a * b / (a + b)


def right(v):
    return pltpu.roll(v, COLS - 1, 1)


def left(v):
    return pltpu.roll(v, 1, 1)


def kernel(
    warm, cls, cond, wn, wt, srow, scol, erow,
    pot, read,
    xbuf, cbuf, ebuf, cond_s, wn_s, wt_s, srow_s, scol_s,
    halo_c, halo_x, packet, slots, surfaces, slots_e,
    chunks, got_first, sums, got_second, mine, slots_r,
    in_sem, halo_send, halo_recv, tile_send, tile_recv,
    first_send, first_recv, second_send, second_recv, r_send, r_recv,
    known,
):
    w = lax.axis_index("wave")
    t = lax.axis_index("tile")

    loads = [
        pltpu.make_async_copy(cls, cbuf, in_sem.at[0]),
        pltpu.make_async_copy(cond, cond_s, in_sem.at[1]),
        pltpu.make_async_copy(warm.at[0], xbuf, in_sem.at[2]),
        pltpu.make_async_copy(wn, wn_s, in_sem.at[3]),
        pltpu.make_async_copy(wt, wt_s, in_sem.at[4]),
        pltpu.make_async_copy(srow, srow_s, in_sem.at[5]),
        pltpu.make_async_copy(scol, scol_s, in_sem.at[6]),
        pltpu.make_async_copy(erow, ebuf, in_sem.at[7]),
    ]
    for load in loads:
        load.start()

    below = lax.rem(t + 1, TILES)
    above = lax.rem(t + TILES - 1, TILES)
    t_y, t_x, t_core = t // 8, lax.rem(t // 2, 4), lax.rem(t, 2)

    def tile_peer(step):
        dy, dx, dc = step
        return (w, lax.rem(t_y + dy, 4) * 8 + lax.rem(t_x + dx, 4) * 2 + lax.rem(t_core + dc, 2))

    def wave_peer(k):
        return (lax.rem(w + 2 * WAVES + k, WAVES), t)

    def tell(semaphore, peers):
        for peer in peers:
            pl.semaphore_signal(semaphore, inc=1, device_id=peer, device_id_type=MESH)

    near = [(w, below), (w, above)] + [tile_peer(s) for s in NEAR] + [wave_peer(1), wave_peer(-1)]
    middle = [tile_peer(s) for s in FAR] + [wave_peer(2), wave_peer(-2)]
    far = [wave_peer(4), wave_peer(-4)]
    barrier = pltpu.get_barrier_semaphore()
    tell(barrier, near)

    def remote(src, dst, send, recv, device):
        return pltpu.make_async_remote_copy(
            src_ref=src, dst_ref=dst, send_sem=send, recv_sem=recv, device_id=device, device_id_type=MESH
        )

    first, final, lower = pl.ds(0, 4), pl.ds(ROWS - 4, 4), pl.ds(4, 4)
    halos = [
        remote(cls.at[first], halo_c.at[0, first], halo_send.at[0], halo_recv.at[0], (w, above)),
        remote(cls.at[final], halo_c.at[1, lower], halo_send.at[1], halo_recv.at[1], (w, below)),
        remote(warm.at[0, :, first], halo_x.at[0, :, first], halo_send.at[2], halo_recv.at[2], (w, above)),
        remote(warm.at[0, :, final], halo_x.at[1, :, lower], halo_send.at[3], halo_recv.at[3], (w, below)),
    ]
    pl.semaphore_wait(barrier, len(near))
    for copy in halos:
        copy.start()
    tell(known.at[0], near)

    def conductivity(classes):
        value = jnp.full(classes.shape, cond_s[0], jnp.float32)
        for i in range(1, 8):
            value = jnp.where(classes == i, cond_s[i], value)
        return value

    for load in loads:
        load.wait()
    sigma = conductivity(cbuf[...])
    pl.semaphore_wait(known.at[0], len(near))
    tell(known.at[1], middle)

    k = wn_s[0]

    def stencil(sig, cell_row, up, down, closed):
        shape = sig.shape
        row = lax.broadcasted_iota(jnp.int32, shape, 0)
        col = lax.broadcasted_iota(jnp.int32, shape, 1)
        last = col == COLS - 1
        face_down = harmonic(sig, down(sig, 0))
        if closed is None:
            face_up = up(face_down, None)
        else:
            face_up = jnp.where(row == closed[0], 0.0, harmonic(sig, up(sig, 0)))
            face_down = jnp.where(row == closed[1], 0.0, face_down)
        face_right = jnp.where(last, 0.0, harmonic(sig, right(sig)))
        face_left = left(face_right)
        diag = face_up + face_down + face_left + face_right + jnp.where(last, sig, 0.0) + (k * k) * sig
        inv = 1.0 / diag
        a_up, a_down, a_left, a_right = face_up * inv, face_down * inv, face_left * inv, face_right * inv

        def apply(v, tag):
            return a_up * up(v, tag) + a_down * down(v, tag) + a_left * left(v) + a_right * right(v)

        def begin(x, s):
            q = jnp.where((cell_row(row) + t * ROWS == srow_s[s]) & (col == scol_s[s]), SOURCE_STRENGTH, 0.0)
            return q * inv - x + apply(x, (s, 0))

        return diag, begin, apply

    def chains(work):
        v0 = [st[1](x, s) for st, x, s in work]
        v1 = [st[2](v, (s, 1)) for (st, _, s), v in zip(work, v0)]
        v2 = [st[2](v, (s, 2)) for (st, _, s), v in zip(work, v1)]
        v3 = [st[2](v, (s, 3)) for (st, _, s), v in zip(work, v2)]
        return list(zip(v0, v1, v2, v3))

    def fold(product):
        total = product[:, :LANES]
        for j in range(1, COLS // LANES):
            total = total + product[:, j * LANES:(j + 1) * LANES]
        return total

    def moments(d, v0, v1, v2, v3):
        d0, d1, d2 = d * v0, d * v1, d * v2
        return [fold(a * b) for a, b in ((d0, v0), (d0, v1), (d1, v1), (d1, v2), (d2, v2), (d2, v3))]

    sub = lax.broadcasted_iota(jnp.int32, (8, COLS), 0)
    upper = sub < 4
    upper_lanes = lax.broadcasted_iota(jnp.int32, (8, LANES), 0) < 4

    whole = stencil(
        sigma,
        lambda row: row,
        lambda v, tag: pltpu.roll(v, 1, 0),
        lambda v, tag: pltpu.roll(v, ROWS - 1, 0),
        None,
    )
    inner = chains([(whole, xbuf[s], s) for s in range(2)])
    inner_moments = [
        [f[8:16] + f[16:24] + jnp.where(upper_lanes, f[24:32], f[0:8]) for f in moments(whole[0], *inner[s])]
        for s in range(2)
    ]
    own = {0: (sigma[0:8], sigma[24:32])}
    for s in range(2):
        own[(s, 0)] = (xbuf[s, 0:8, :], xbuf[s, 24:32, :])
        for i in range(3):
            own[(s, i + 1)] = (inner[s][i][0:8], inner[s][i][24:32])

    electrode = ebuf[...].reshape(1, 64)
    electrode = jnp.concatenate([electrode, electrode], axis=1)
    here = lax.broadcasted_iota(jnp.int32, (ROWS, LANES), 0) + t * ROWS == electrode

    for copy in halos:
        copy.wait_recv()
    pl.semaphore_wait(known.at[1], len(middle))
    tell(known.at[2], far)

    edge_stencil = [
        stencil(
            jnp.where(upper, sigma[0:8], conductivity(halo_c[1])),
            lambda row: jnp.where(row < 4, row, row - 8),
            lambda v, tag: pltpu.roll(v, 1, 0),
            lambda v, tag: pltpu.roll(jnp.where(sub == 4, own[tag][0], v), 7, 0),
            (jnp.where(t == 0, 0, -1), jnp.where(t == 0, 7, -1)),
        ),
        stencil(
            jnp.where(upper, conductivity(halo_c[0]), sigma[24:32]),
            lambda row: jnp.where(row < 4, row + 32, row + 24),
            lambda v, tag: pltpu.roll(jnp.where(sub == 3, own[tag][1], v), 1, 0),
            lambda v, tag: pltpu.roll(v, 7, 0),
            (jnp.where(t == TILES - 1, 0, -1), jnp.where(t == TILES - 1, 7, -1)),
        ),
    ]
    outer = chains(
        [(edge_stencil[0], jnp.where(upper, own[(s, 0)][0], halo_x[1, s]), s) for s in range(2)]
        + [(edge_stencil[1], jnp.where(upper, halo_x[0, s], own[(s, 0)][1]), s) for s in range(2)]
    )
    edges = [(outer[s], outer[2 + s]) for s in range(2)]
    rows = []
    for s in range(2):
        pairs = zip(moments(edge_stencil[0][0], *edges[s][0]), moments(edge_stencil[1][0], *edges[s][1]))
        rows += [
            jnp.sum(a + jnp.where(upper_lanes, b, c), axis=0, keepdims=True)
            for a, (b, c) in zip(inner_moments[s], pairs)
        ]

    dots = jnp.sum(jnp.concatenate(rows, axis=0), axis=1, keepdims=True)
    eye = lax.broadcasted_iota(jnp.int32, (12, LANES), 0) == lax.broadcasted_iota(jnp.int32, (12, LANES), 1)
    packet[...] = jnp.sum(jnp.where(eye, dots, 0.0), axis=0, keepdims=True)
    peers = [tile_peer(step) for step in STEPS]
    for i, peer in enumerate(peers):
        remote(packet, slots.at[i], tile_send.at[0], tile_recv.at[0], peer).start()
    vectors = [
        [xbuf[s]]
        + [
            jnp.concatenate(
                [
                    jnp.where(upper, edges[s][0][i], inner[s][i][0:8]),
                    inner[s][i][8:24],
                    jnp.where(upper, inner[s][i][24:32], edges[s][1][i]),
                ],
                axis=0,
            )
            for i in range(3)
        ]
        for s in range(2)
    ]
    lane = lax.broadcasted_iota(jnp.int32, (1, LANES), 1)
    low = lane < 64
    surface = []
    for i in range(4):
        both = jnp.where(low, vectors[0][i][:, 0:1], vectors[1][i][:, 0:1])
        surface.append(jnp.sum(jnp.where(here, both, 0.0), axis=0, keepdims=True))
    surfaces[...] = jnp.concatenate(surface, axis=0)
    for i, peer in enumerate(peers):
        remote(surfaces, slots_e.at[i], tile_send.at[1], tile_recv.at[1], peer).start()

    every = remote(slots, slots, tile_send.at[0], tile_recv.at[0], (w, below))
    every_e = remote(slots_e, slots_e, tile_send.at[1], tile_recv.at[1], (w, below))
    every.wait_recv()
    total = packet[...] + jnp.sum(slots[...], axis=0)
    pl.semaphore_wait(known.at[2], len(far))

    weight = wt_s[0]
    coefs = []
    for s in range(2):
        nu = [jnp.broadcast_to(total[0:1, 6 * s + m:6 * s + m + 1], (1, LANES)) for m in range(6)]
        mu = [nu[m] - nu[m + 1] for m in range(5)]
        gamma0 = nu[0]
        alpha0 = gamma0 / mu[0]
        za, zb = 1.0 - alpha0, alpha0
        gamma1 = za * za * nu[0] + 2.0 * za * zb * nu[1] + zb * zb * nu[2]
        beta0 = gamma1 / gamma0
        pa, pb = za + beta0, zb
        curve1 = pa * pa * mu[0] + 2.0 * pa * pb * mu[1] + pb * pb * mu[2]
        alpha1 = gamma1 / curve1
        ya, yb, yc = za - alpha1 * pa, zb - alpha1 * (pb - pa), alpha1 * pb
        gamma2 = (
            ya * ya * nu[0] + yb * yb * nu[2] + yc * yc * nu[4]
            + 2.0 * (ya * yb * nu[1] + ya * yc * nu[2] + yb * yc * nu[3])
        )
        beta1 = gamma2 / gamma1
        ra, rb, rc = ya + beta1 * pa, yb + beta1 * pb, yc
        curve2 = (
            ra * ra * mu[0] + rb * rb * mu[2] + rc * rc * mu[4]
            + 2.0 * (ra * rb * mu[1] + ra * rc * mu[2] + rb * rc * mu[3])
        )
        alpha2 = gamma2 / curve2
        coefs.append((
            jnp.full((1, LANES), weight, jnp.float32),
            weight * (alpha0 + alpha1 * pa + alpha2 * ra),
            weight * (alpha1 * pb + alpha2 * rb),
            weight * (alpha2 * rc),
        ))

    low_rows = lax.broadcasted_iota(jnp.int32, (ROWS, LANES), 1) < 64
    for j in range(COLS // LANES):
        part = []
        for s in range(2):
            acc = vectors[s][0][:, j * LANES:(j + 1) * LANES] * coefs[s][0]
            for i in range(1, 4):
                acc = acc + vectors[s][i][:, j * LANES:(j + 1) * LANES] * coefs[s][i]
            part.append(acc)
        chunks[2 * j] = jnp.where(low_rows, part[0], pltpu.roll(part[1], 64, 1))
        chunks[2 * j + 1] = jnp.where(low_rows, pltpu.roll(part[0], 64, 1), part[1])

    copies_first = [
        remote(
            chunks.at[wave_peer(-o)[0]], got_first.at[i], first_send.at[i], first_recv.at[i], wave_peer(c - o)
        )
        for i, (c, o) in enumerate(FIRST_LIST)
    ]
    for copy in copies_first:
        copy.start()
    every_e.wait_recv()
    total_e = surfaces[...] + jnp.sum(slots_e[...], axis=0)
    mine[...] = sum(total_e[i:i + 1] * jnp.where(low, coefs[0][i], coefs[1][i]) for i in range(4))
    copies_r = [remote(mine, slots_r.at[i], r_send, r_recv, wave_peer(i + 1)) for i in range(WAVES - 1)]
    order = sorted(range(WAVES - 1), key=lambda i: -min(i + 1, WAVES - 1 - i))
    for i in order[:N_FAR_R]:
        copies_r[i].start()

    for i in order[N_FAR_R:]:
        copies_r[i].start()

    copies_second = []
    for j, c in enumerate(SECOND_LIST):
        acc = chunks[wave_peer(-c)[0]]
        for i, (cc, o) in enumerate(FIRST_LIST):
            if cc == c:
                copies_first[i].wait_recv()
                acc = acc + got_first[i]
        sums[j] = acc
        copy = remote(sums.at[j], got_second.at[j], second_send.at[j], second_recv.at[j], wave_peer(-c))
        copy.start()
        copies_second.append(copy)
    every_r = remote(slots_r, slots_r, r_send, r_recv, wave_peer(1))

    acc = chunks[w]
    for i, (c, o) in enumerate(FIRST_LIST):
        if c == 0:
            copies_first[i].wait_recv()
            acc = acc + got_first[i]
    for j in reversed(range(len(SECOND_LIST))):
        copies_second[j].wait_recv()
        acc = acc + got_second[j]
    pot[...] = acc

    every_r.wait_recv()
    read[...] = mine[...] + jnp.sum(slots_r[...], axis=0)

    for copy in halos + [every, every_e, every_r] + copies_first + copies_second:
        copy.wait_send()


def part(both, both_r, pot, read):
    pot[0] = both[:, :64]
    pot[1] = both[:, 64:]
    read[0:1, :] = both_r[:, :64]
    read[1:2, :] = both_r[:, 64:]


def shards(warm, cls, cond, wn, wt, srow, scol, erow):
    f32 = jnp.float32
    in_vmem = pl.BlockSpec(memory_space=pltpu.VMEM)
    dma = pltpu.SemaphoreType.DMA
    n_first, n_second = len(FIRST_LIST), len(SECOND_LIST)
    both = pl.pallas_call(
        kernel,
        out_shape=(
            jax.ShapeDtypeStruct((ROWS, LANES), f32),
            jax.ShapeDtypeStruct((1, LANES), f32),
        ),
        in_specs=[pl.BlockSpec(memory_space=pltpu.HBM)] * 8,
        out_specs=[in_vmem] * 2,
        scratch_shapes=[
            pltpu.VMEM((2, ROWS, COLS), f32),
            pltpu.VMEM((ROWS, COLS), jnp.int32),
            pltpu.VMEM((64,), jnp.int32),
            pltpu.SMEM((8,), f32),
            pltpu.SMEM((1,), f32),
            pltpu.SMEM((1,), f32),
            pltpu.SMEM((2,), jnp.int32),
            pltpu.SMEM((2,), jnp.int32),
            pltpu.VMEM((2, 8, COLS), jnp.int32),
            pltpu.VMEM((2, 2, 8, COLS), f32),
            pltpu.VMEM((1, LANES), f32),
            pltpu.VMEM((TILES - 1, 1, LANES), f32),
            pltpu.VMEM((4, LANES), f32),
            pltpu.VMEM((TILES - 1, 4, LANES), f32),
            pltpu.VMEM((WAVES, ROWS, LANES), f32),
            pltpu.VMEM((n_first, ROWS, LANES), f32),
            pltpu.VMEM((n_second, ROWS, LANES), f32),
            pltpu.VMEM((n_second, ROWS, LANES), f32),
            pltpu.VMEM((1, LANES), f32),
            pltpu.VMEM((WAVES - 1, 1, LANES), f32),
            dma((8,)),
            dma((4,)), dma((4,)),
            dma((2,)), dma((2,)),
            dma((n_first,)), dma((n_first,)),
            dma((n_second,)), dma((n_second,)),
            dma, dma,
            pltpu.SemaphoreType.REGULAR((3,)),
        ],
        compiler_params=pltpu.CompilerParams(
            collective_id=0, has_side_effects=True, vmem_limit_bytes=55168 * 1024
        ),
    )(warm, cls, cond, wn, wt, srow, scol, erow)
    return pl.pallas_call(
        part,
        out_shape=(
            jax.ShapeDtypeStruct((2, ROWS, COLS // WAVES), f32),
            jax.ShapeDtypeStruct((2, 64), f32),
        ),
        in_specs=[in_vmem] * 2,
        out_specs=[in_vmem] * 2,
        compiler_params=pltpu.CompilerParams(vmem_limit_bytes=55168 * 1024),
    )(*both)


def solution(mesh):
    return jax.shard_map(
        shards,
        mesh=mesh,
        in_specs=(
            P("wave", None, "tile", None), P("tile", None), P(), P("wave"), P("wave"), P(), P(), P(),
        ),
        out_specs=(P(None, "tile", "wave"), P()),
        check_vma=False,
    )
```
